32 devices in a mesh: section: 8 (over z, y), dp: 2 (over x), mp: 2 (over core).
Axes of the slice: x: 2, y: 2, z: 4, core: 2. Of those that a mesh axis runs over, the one named last changes fastest.
Arguments:
- old_w: float32 [8, 2, 8, 208, 3328], P(None, 'dp', 'section', None, 'mp'), may hold values from -0.109375 to 0.109375
- old_m: bfloat16 [8, 2, 8, 208, 3328], P(None, 'dp', 'section', None, 'mp'), may hold values from -12 to 12
- old_v: bfloat16 [8, 2, 8, 208, 3328], P(None, 'dp', 'section', None, 'mp'), may hold values from 0.5 to 20
- old_slot_layer: int32 [8], replicated, may hold values from 0 to 7, each once
- norm_gain: float32 [8, 3328], P('section'), may hold values from 0.5 to 2
- tokens: bfloat16 [8, 32, 3328], P(None, 'dp'), may hold values from -6 to 6
- cotangent: bfloat16 [8, 32, 3328], P(None, 'dp'), may hold values from -6 to 6
Outputs:
- new_w: float32 [8, 3328, 3328], P('section', 'dp', 'mp')
- new_m: bfloat16 [8, 3328, 3328], P('section', 'dp', 'mp')
- new_v: bfloat16 [8, 3328, 3328], P('section', 'dp', 'mp')
The draws below stay inside these ranges and needn't reach their ends.
Inputs may be any that keep to these rules, and one draw needn't show every extreme that they name: `old_slot_layer`: every layer number appears exactly once.
All inputs are finite; a program needn't handle non-finite values.
Results may differ from the reference program's by a relative error of at most 0.028.
Values may be sent and summed in bfloat16 or wider, within the bound.
No kernel may reach another device: no remote copies, remote signals or barrier semaphores. Data moves between devices by JAX's collectives and lax.ppermute only.
A program may use at most 128 MiB of HBM per device.

```python
import math
import jax
import jax.numpy as jnp
from jax import lax

E = 3328
MB = 8
LAYERS = 8
PR = 208
TOKENS = 32
N_SECTION = 8
N_DP = 2


def block_scale(key, extent, cuts, least, high):
    level, own = 1.0, jax.random.fold_in(key, 6)
    for dim, parts in cuts:
        heights = jnp.exp(jax.random.uniform(jax.random.fold_in(own, dim), (parts,), jnp.float32, least / len(cuts), high / len(cuts)))
        level = level * jnp.repeat(heights, extent[dim] // parts).reshape([-1 if axis == dim else 1 for axis in range(len(extent))])
    return level


def centred(stream_key, shape, scale, reach, shards=(), held_as=jnp.bfloat16):
    gain = block_scale(stream_key, shape, shards, -0.22, 0.18) if shards else 1.0
    result = jax.random.normal(stream_key, shape, jnp.float32) * scale * gain
    return jnp.minimum(jnp.maximum(result, -reach), reach).astype(held_as)


def setup_inputs(seed: int = 0) -> dict:
    key_of = jax.random.split(jax.random.key(seed), 8)
    return {
        "old_w": centred(key_of[0], (LAYERS, N_DP, N_SECTION, PR, E), E ** -0.5, 0.109375, ((1, 2), (2, 8), (4, 2)), jnp.float32),
        "old_m": centred(key_of[1], (LAYERS, N_DP, N_SECTION, PR, E), 2.0, 12.0, ((1, 2), (2, 8), (4, 2))),
        "old_v": jnp.clip(jnp.exp(math.log(20.0) - 3.6888795 * jax.random.uniform(key_of[2], (LAYERS, N_DP, N_SECTION, PR, E), jnp.float32) ** block_scale(key_of[2], (LAYERS, N_DP, N_SECTION, PR, E), ((1, 2), (2, 8), (4, 2)), -0.2, 0.2)), 0.5, 20.0).astype(jnp.bfloat16),
        "old_slot_layer": jax.random.permutation(key_of[3], LAYERS).astype(jnp.int32),
        "norm_gain": jnp.clip(jnp.exp(math.log(2.0) - 1.3862944 * jax.random.uniform(key_of[4], (LAYERS, E), jnp.float32) ** block_scale(key_of[4], (LAYERS, E), ((0, 8),), -0.2, 0.2)), 0.5, 2.0),
        "tokens": centred(key_of[5], (MB, TOKENS, E), 1.0, 6.0, ((1, 2),)),
        "cotangent": centred(key_of[6], (MB, TOKENS, E), 1.0, 6.0, ((1, 2),)),
    }


eps_norm = 1e-05
beta_one = 0.9
beta_two = 0.95
learn_rate = 0.001
decay_rate = 0.1
adam_eps = 1e-08
step_count = 1000.0

def silu_slope(values):
    sigmoid_value = jax.nn.sigmoid(values)
    return sigmoid_value * (1.0 + values * (1.0 - sigmoid_value))

def row_scale_of(inputs):
    widened = inputs.astype(jnp.float32)
    return lax.rsqrt(lax.optimization_barrier(jnp.mean(widened * widened, axis=1, keepdims=True)) + eps_norm)

def reference(old_w, old_m, old_v, old_slot_layer, norm_gain, tokens, cotangent):
    layer_total = old_w.shape[0]
    full_width = old_w.shape[-1]
    layer_ids = jnp.arange(layer_total, dtype=jnp.int32)
    matches = (old_slot_layer[None, :] == layer_ids[:, None]).astype(jnp.int32)
    inverse = lax.optimization_barrier(jnp.sum(matches * layer_ids[None, :], axis=1)).astype(jnp.int32)
    master = jnp.take(old_w.reshape(layer_total, full_width, full_width), inverse, axis=0)
    first_moment = jnp.take(old_m.reshape(layer_total, full_width, full_width), inverse, axis=0)
    second_moment = jnp.take(old_v.reshape(layer_total, full_width, full_width), inverse, axis=0)
    current = tokens.reshape(-1, full_width)
    stashed = []
    normed_list = []
    preact_list = []
    for layer in range(layer_total):
        weight_copy = master[layer].astype(jnp.bfloat16)
        widened = current.astype(jnp.float32)
        row_scale = row_scale_of(current)
        normed = (widened * row_scale * norm_gain[layer]).astype(jnp.bfloat16)
        preact = jnp.dot(normed, weight_copy, preferred_element_type=jnp.float32)
        stashed.append(current)
        normed_list.append(normed)
        preact_list.append(preact)
        current = (widened + jax.nn.silu(preact)).astype(jnp.bfloat16)
    back_grad = cotangent.reshape(-1, full_width)
    weights_out = []
    firsts_out = []
    seconds_out = []
    for layer in range(layer_total - 1, -1, -1):
        weight_copy = master[layer].astype(jnp.bfloat16)
        dpre = (back_grad.astype(jnp.float32) * silu_slope(preact_list[layer])).astype(jnp.bfloat16)
        weight_grad = jnp.dot(normed_list[layer].T, dpre, preferred_element_type=jnp.float32)
        dnormed = lax.dot_general(dpre, weight_copy, (((1,), (1,)), ((), ())), preferred_element_type=jnp.float32)
        inputs = stashed[layer]
        widened = inputs.astype(jnp.float32)
        row_scale = row_scale_of(inputs)
        weighted = norm_gain[layer] * dnormed
        row_stat = lax.optimization_barrier(jnp.mean(widened * weighted, axis=1, keepdims=True))
        cube = row_scale * row_scale * row_scale
        back_grad = (back_grad.astype(jnp.float32) + row_scale * weighted - widened * cube * row_stat).astype(jnp.bfloat16)
        moment_next = beta_one * first_moment[layer].astype(jnp.float32) + (1.0 - beta_one) * weight_grad
        second_next = beta_two * second_moment[layer].astype(jnp.float32) + (1.0 - beta_two) * weight_grad * weight_grad
        fix_one = 1.0 - beta_one ** step_count
        fix_two = 1.0 - beta_two ** step_count
        direction = moment_next / fix_one / (jnp.sqrt(second_next / fix_two) + adam_eps)
        weights_out.append(master[layer] - learn_rate * (direction + decay_rate * master[layer]))
        firsts_out.append(moment_next.astype(jnp.bfloat16))
        seconds_out.append(second_next.astype(jnp.bfloat16))
    new_w = jnp.stack(weights_out[::-1], axis=0)
    new_m = jnp.stack(firsts_out[::-1], axis=0)
    new_v = jnp.stack(seconds_out[::-1], axis=0)
    return (new_w, new_m, new_v)
```

```python
import jax
import jax.numpy as jnp
from jax import lax
from jax.experimental import pallas as pl
from jax.experimental.pallas import tpu as pltpu
from jax.sharding import PartitionSpec as P

eps_norm = 1e-05
beta_one = 0.9
beta_two = 0.95
learn_rate = 0.001
decay_rate = 0.1
adam_eps = 1e-08
step_count = 1000.0

GROUPS = 2
CHUNKS = 2
KERNEL_VMEM = 24 * 1024 * 1024


def turn(value, axis, by):
    count = lax.axis_size(axis)
    return lax.ppermute(value, axis, [(i, (i + by) % count) for i in range(count)])


def after(value, *others):
    return lax.optimization_barrier((value,) + others)[0]


def relocate(pieces):
    moved = lax.all_to_all(pieces, "section", split_axis=0, concat_axis=2, tiled=True)
    return moved.reshape(-1, moved.shape[-1])


def column_cuts(width, parts):
    lanes = width // 128
    edges = [lanes * i // parts * 128 for i in range(parts)] + [width]
    return list(zip(edges[:-1], edges[1:]))


def ordered_cast(inverse, pieces, cuts):
    slots, _, _, rows, width = pieces.shape

    def body(order_ref, in_ref, *out_refs):
        for (lo, hi), out_ref in zip(cuts, out_refs):
            out_ref[...] = in_ref[:, :, :, :, lo:hi].astype(out_ref.dtype)

    def place(i, order_ref):
        return (i, 0, 0, 0, 0)

    return pl.pallas_call(
        body,
        out_shape=[
            jax.ShapeDtypeStruct((slots, 1, 1, rows, hi - lo), jnp.bfloat16) for lo, hi in cuts
        ],
        grid_spec=pltpu.PrefetchScalarGridSpec(
            num_scalar_prefetch=1,
            grid=(slots,),
            in_specs=[pl.BlockSpec((1, 1, 1, rows, width), lambda i, o: (o[i], 0, 0, 0, 0))],
            out_specs=[pl.BlockSpec((1, 1, 1, rows, hi - lo), place) for lo, hi in cuts],
        ),
        compiler_params=pltpu.CompilerParams(vmem_limit_bytes=KERNEL_VMEM),
    )(inverse, pieces)


def adam(features, dpre, master, moment_one, moment_two, row_tile):
    rows, width = moment_one.shape
    depth = dpre.shape[0]
    fix_one = 1.0 - beta_one**step_count
    fix_two = 1.0 - beta_two**step_count

    def body(feature_ref, dpre_ref, w_ref, m_ref, v_ref, new_w_ref, new_m_ref, new_v_ref):
        grad = lax.dot_general(
            feature_ref[...],
            dpre_ref[...],
            (((0,), (0,)), ((), ())),
            preferred_element_type=jnp.float32,
        )
        moment_next = beta_one * m_ref[...].astype(jnp.float32) + (1.0 - beta_one) * grad
        second_next = beta_two * v_ref[...].astype(jnp.float32) + (1.0 - beta_two) * grad * grad
        direction = moment_next / fix_one / (jnp.sqrt(second_next / fix_two) + adam_eps)
        master_rows = w_ref[...].astype(jnp.float32)
        new_w_ref[...] = master_rows - learn_rate * (direction + decay_rate * master_rows)
        new_m_ref[...] = moment_next.astype(jnp.bfloat16)
        new_v_ref[...] = second_next.astype(jnp.bfloat16)

    tile = pl.BlockSpec((row_tile, width), lambda i: (i, 0))
    return pl.pallas_call(
        body,
        grid=(rows // row_tile,),
        in_specs=[
            pl.BlockSpec((depth, row_tile), lambda i: (0, i)),
            pl.BlockSpec((depth, width), lambda i: (0, 0)),
            tile,
            tile,
            tile,
        ],
        out_specs=[tile, tile, tile],
        out_shape=[
            jax.ShapeDtypeStruct((rows, width), jnp.float32),
            jax.ShapeDtypeStruct((rows, width), jnp.bfloat16),
            jax.ShapeDtypeStruct((rows, width), jnp.bfloat16),
        ],
        compiler_params=pltpu.CompilerParams(vmem_limit_bytes=KERNEL_VMEM),
    )(features, dpre, master, moment_one, moment_two)


def local(old_w, old_m, old_v, old_slot_layer, norm_gain, tokens, cotangent):
    sections = lax.axis_size("section")
    replicas = lax.axis_size("dp")
    cores = lax.axis_size("mp")
    section_index = lax.axis_index("section")
    replica_index = lax.axis_index("dp")
    core_index = lax.axis_index("mp")
    full_width = tokens.shape[2]
    half_width = old_w.shape[4]
    row_block = sections * old_w.shape[3]
    tokens = tokens.reshape(-1, full_width)
    cotangent = cotangent.reshape(-1, full_width)
    token_total = tokens.shape[0]
    group_rows = token_total // GROUPS
    layer_ids = jnp.arange(sections, dtype=jnp.int32)
    matches = (old_slot_layer[None, :] == layer_ids[:, None]).astype(jnp.int32)
    inverse = jnp.sum(matches * layer_ids[None, :], axis=1)
    cuts = column_cuts(half_width, CHUNKS)

    own_w = [relocate(piece) for piece in ordered_cast(inverse, old_w, cuts)]
    weight = [lax.all_gather(piece, "dp", axis=0, tiled=True) for piece in own_w]
    ordered_m = jnp.take(old_m, after(inverse, own_w[0]), axis=0)
    moment_one = relocate(after(ordered_m, own_w[-1]))
    ordered_v = jnp.take(old_v, after(inverse, own_w[-1]), axis=0)
    moment_two = relocate(after(ordered_v, moment_one))
    weight = lax.optimization_barrier(jnp.concatenate(weight, axis=1))
    master = lax.optimization_barrier(jnp.concatenate(own_w, axis=1))

    gain_row = norm_gain[0]

    def half_of(value, by=0):
        start = lax.rem(core_index + by, cores) * half_width
        return lax.dynamic_slice_in_dim(value, start, half_width, value.ndim - 1)

    turned = [
        lax.optimization_barrier(
            lax.dynamic_slice_in_dim(
                weight, lax.rem(core_index + by, cores) * half_width, half_width, 0
            ).T
        )
        for by in range(cores)
    ]
    tokens = after(tokens, moment_two)

    def row_scale_of(inputs):
        widened = inputs.astype(jnp.float32)
        return lax.rsqrt(jnp.mean(widened * widened, axis=1, keepdims=True) + eps_norm)

    def normed_of(inputs):
        return (inputs.astype(jnp.float32) * row_scale_of(inputs) * gain_row).astype(jnp.bfloat16)

    def put(stash, value, slot):
        return lax.dynamic_update_index_in_dim(stash, value, slot, 0)

    def get(stash, slot):
        return lax.dynamic_index_in_dim(stash, slot, 0, keepdims=False)

    def slot_of(group):
        return jnp.where((group >= 0) & (group < GROUPS), group, GROUPS)

    def hop(value, tick, by):
        senders = [tick - group for group in range(GROUPS) if 0 <= tick - group < sections - 1]
        pairs = [(s, s + 1) for s in senders]
        if by < 0:
            pairs = [(sections - 1 - s, sections - 2 - s) for s in senders]
        return lax.ppermute(value, "section", pairs)

    acts = jnp.zeros((GROUPS + 1, group_rows, full_width), jnp.bfloat16)
    preacts = jnp.zeros((GROUPS + 1, group_rows, half_width), jnp.float32)
    ticks = GROUPS + sections - 1
    arriving = jnp.zeros((group_rows, full_width), jnp.bfloat16)
    for tick in range(ticks):
        slot = slot_of(tick - section_index)
        inputs = arriving
        if tick < GROUPS:
            entry = tokens[tick * group_rows : (tick + 1) * group_rows]
            inputs = jnp.where(section_index == 0, entry, arriving)
        preact = jnp.dot(normed_of(inputs), weight, preferred_element_type=jnp.float32)
        acts = put(acts, inputs, slot)
        preacts = put(preacts, preact, slot)
        if tick < ticks - 1:
            output = (half_of(inputs).astype(jnp.float32) + jax.nn.silu(preact)).astype(
                jnp.bfloat16
            )
            moved = hop(output, tick, 1)
            arriving = lax.all_gather(moved, "mp", axis=1, tiled=True)

    normed_all = normed_of(acts[:GROUPS].reshape(token_total, full_width))
    features = []
    for by in range(replicas):
        block = lax.rem(replica_index + by, replicas) * row_block
        part = lax.dynamic_slice_in_dim(normed_all, block, row_block, 1)
        features.append(turn(part, "dp", by) if by else part)
    features = jnp.concatenate(features, axis=0)

    sigmoid_value = jax.nn.sigmoid(preacts)
    slopes = lax.optimization_barrier(
        sigmoid_value * (1.0 + preacts * (1.0 - sigmoid_value))
    )
    dpres = jnp.zeros((GROUPS + 1, group_rows, half_width), jnp.bfloat16)
    arriving = jnp.zeros((group_rows, half_width), jnp.bfloat16)
    for tick in range(ticks):
        slot = slot_of(tick - (sections - 1 - section_index))
        slope = get(slopes, slot)
        preact = get(preacts, slot)
        inputs = get(acts, slot)
        row_scale = row_scale_of(inputs)
        scaled = [half_of(gain_row, by) * row_scale for by in range(cores)]
        pulled = [
            half_of(inputs, by).astype(jnp.float32) * (row_scale * row_scale / full_width)
            for by in range(cores)
        ]
        slope, preact, scaled, pulled = lax.optimization_barrier((slope, preact, scaled, pulled))
        upstream = arriving
        if tick < GROUPS:
            seed = cotangent[tick * group_rows : (tick + 1) * group_rows]
            upstream = jnp.where(section_index == sections - 1, half_of(seed), arriving)
        dpre = (upstream.astype(jnp.float32) * slope).astype(jnp.bfloat16)
        dpres = put(dpres, dpre, slot)
        if tick == ticks - 1:
            break
        stat = jnp.sum(dpre.astype(jnp.float32) * preact, axis=1, keepdims=True)
        total = upstream.astype(jnp.float32)
        for by in reversed(range(cores)):
            part = (
                scaled[by] * jnp.dot(dpre, turned[by], preferred_element_type=jnp.float32)
                - pulled[by] * stat
            )
            if by:
                part = turn(part.astype(jnp.bfloat16), "mp", by).astype(jnp.float32)
            total = total + part
        arriving = hop(total.astype(jnp.bfloat16), tick, -1)

    dpre_all = dpres[:GROUPS].reshape(token_total, half_width)
    dpre_all = jnp.concatenate(
        [turn(dpre_all, "dp", by) if by else dpre_all for by in range(replicas)], axis=0
    )
    row_tile = 128 if row_block % 128 == 0 else row_block
    updated = adam(features, dpre_all, master, moment_one, moment_two, row_tile)
    return tuple(value[None] for value in updated)


def solution(mesh):
    placed = (
        P(None, "dp", "section", None, "mp"),
        P(None, "dp", "section", None, "mp"),
        P(None, "dp", "section", None, "mp"),
        P(),
        P("section", None),
        P(None, "dp", None),
        P(None, "dp", None),
    )
    return jax.shard_map(
        local,
        mesh=mesh,
        in_specs=placed,
        out_specs=(P("section", "dp", "mp"), P("section", "dp", "mp"), P("section", "dp", "mp")),
        check_vma=False,
    )
```

```python
import jax
import jax.numpy as jnp
from jax import lax
from jax.experimental import pallas as pl
from jax.experimental.pallas import tpu as pltpu
from jax.sharding import PartitionSpec as P

eps_norm = 1e-05
beta_one = 0.9
beta_two = 0.95
learn_rate = 0.001
decay_rate = 0.1
adam_eps = 1e-08
step_count = 1000.0

GROUPS = 2
EARLY = 2
STEP_VMEM = 16 * 1024 * 1024
ADAM_VMEM = 20 * 1024 * 1024


def turn(value, axis, by):
    count = lax.axis_size(axis)
    return lax.ppermute(value, axis, [(i, (i + by) % count) for i in range(count)])


def zero_after(value):
    first = lax.slice(value, (0,) * value.ndim, (1,) * value.ndim).reshape(())
    return jnp.minimum((first > 0).astype(jnp.int32), 0)


def relocate(pieces):
    moved = lax.all_to_all(pieces, "section", split_axis=0, concat_axis=2, tiled=True)
    return moved.reshape(-1, moved.shape[-1])


def ordered_copy(picks, pieces):
    slots, _, _, rows, width = pieces.shape

    def body(pick_ref, in_ref, out_ref):
        out_ref[...] = in_ref[...].astype(out_ref.dtype)

    return pl.pallas_call(
        body,
        out_shape=jax.ShapeDtypeStruct((picks.shape[0], 1, 1, rows, width), jnp.bfloat16),
        grid_spec=pltpu.PrefetchScalarGridSpec(
            num_scalar_prefetch=1,
            grid=(picks.shape[0],),
            in_specs=[pl.BlockSpec((1, 1, 1, rows, width), lambda i, p: (p[i], 0, 0, 0, 0))],
            out_specs=pl.BlockSpec((1, 1, 1, rows, width), lambda i, p: (i, 0, 0, 0, 0)),
        ),
        compiler_params=pltpu.CompilerParams(vmem_limit_bytes=STEP_VMEM),
    )(picks, pieces)


def resident(array):
    def body(in_ref, out_ref, sem):
        copy = pltpu.make_async_copy(in_ref, out_ref, sem)
        copy.start()
        copy.wait()

    return pl.pallas_call(
        body,
        out_shape=pltpu.VMEM(array.shape, array.dtype),
        in_specs=[pl.BlockSpec(memory_space=pl.ANY)],
        out_specs=pl.BlockSpec(memory_space=pltpu.VMEM),
        scratch_shapes=[pltpu.SemaphoreType.DMA],
        compiler_params=pltpu.CompilerParams(vmem_limit_bytes=STEP_VMEM),
    )(in_hbm(array))


def picked_pieces(picks, pieces):
    _, _, _, rows, width = pieces.shape
    count = picks.shape[0]

    def body(pick_ref, in_ref, *refs):
        out_refs, sems = refs[:count], refs[count]
        copies = [
            pltpu.make_async_copy(in_ref.at[pick_ref[i], 0, 0], out_refs[i], sems.at[i])
            for i in range(count)
        ]
        for copy in copies:
            copy.start()
        for copy in copies:
            copy.wait()

    return pl.pallas_call(
        body,
        out_shape=[jax.ShapeDtypeStruct((rows, width), pieces.dtype)] * count,
        in_specs=[pl.BlockSpec(memory_space=pltpu.SMEM), pl.BlockSpec(memory_space=pl.ANY)],
        out_specs=[pl.BlockSpec(memory_space=pl.ANY)] * count,
        scratch_shapes=[pltpu.SemaphoreType.DMA((count,))],
        compiler_params=pltpu.CompilerParams(vmem_limit_bytes=STEP_VMEM),
    )(picks, pieces)


def tiles_of(width):
    return [(start, min(256, width - start)) for start in range(0, width, 256)]


def in_vmem(array):
    return pltpu.with_memory_space_constraint(array, pltpu.VMEM)


def in_hbm(array):
    return pltpu.with_memory_space_constraint(array, pltpu.HBM)


WHOLE = pl.BlockSpec(memory_space=pltpu.VMEM)
SCALAR = pl.BlockSpec(memory_space=pltpu.SMEM)
ANYWHERE = pl.BlockSpec(memory_space=pl.ANY)


def forward_step(core, inputs, gain, weight):
    rows, full_width = inputs.shape
    half_width = weight.shape[1]

    def body(core_ref, x_ref, gain_ref, w_ref, out_ref, normed_ref, preact_ref, scale_ref, _):
        wide = x_ref[...].astype(jnp.float32)
        scale = lax.rsqrt(jnp.mean(wide * wide, axis=1, keepdims=True) + eps_norm)
        normed = (wide * scale * gain_ref[...]).astype(jnp.bfloat16)
        normed_ref[...] = normed
        scale_ref[...] = jnp.broadcast_to(scale, scale_ref.shape)
        offset = pl.multiple_of(core_ref[0] * half_width, 128)
        for start, size in tiles_of(half_width):
            preact = jnp.dot(
                normed, w_ref[:, start : start + size], preferred_element_type=jnp.float32
            )
            preact_ref[:, start : start + size] = preact
            own = x_ref[:, pl.ds(pl.multiple_of(offset + start, 128), size)].astype(jnp.float32)
            silu = preact / (1.0 + jnp.exp(-preact))
            out_ref[:, start : start + size] = (own + silu).astype(jnp.bfloat16)

    return pl.pallas_call(
        body,
        in_specs=[SCALAR, WHOLE, WHOLE, WHOLE],
        out_specs=[WHOLE] * 5,
        out_shape=[
            jax.ShapeDtypeStruct((rows, half_width), jnp.bfloat16),
            jax.ShapeDtypeStruct((rows, full_width), jnp.bfloat16),
            jax.ShapeDtypeStruct((rows, half_width), jnp.float32),
            jax.ShapeDtypeStruct((rows, 128), jnp.float32),
            pltpu.VMEM(weight.shape, weight.dtype),
        ],
        input_output_aliases={3: 4},
        compiler_params=pltpu.CompilerParams(vmem_limit_bytes=STEP_VMEM),
    )(core, inputs, gain, in_vmem(weight))


def pull_back(start, dpre, stat, w_ref, x_ref, gain_ref, scale_ref, size, width):
    cols = pl.ds(pl.multiple_of(start, 128), size)
    product = lax.dot_general(
        dpre, w_ref[cols, :], (((1,), (1,)), ((), ())), preferred_element_type=jnp.float32
    )
    scale = scale_ref[:, :1]
    return scale * (
        gain_ref[:, cols] * product - x_ref[:, cols].astype(jnp.float32) * (scale * stat / width)
    )


def backward_away(core, upstream, slope, preact, inputs, row_scale, gain, weight):
    rows, full_width = inputs.shape
    half_width = weight.shape[1]

    def body(
        core_ref, up_ref, slope_ref, preact_ref, x_ref, scale_ref, gain_ref, w_ref,
        dpre_ref, stat_ref, away_ref, _,
    ):
        dpre = (up_ref[...].astype(jnp.float32) * slope_ref[...]).astype(jnp.bfloat16)
        dpre_ref[...] = dpre
        stat = jnp.sum(dpre.astype(jnp.float32) * preact_ref[...], axis=1, keepdims=True)
        stat_ref[...] = jnp.broadcast_to(stat, stat_ref.shape)
        offset = pl.multiple_of(core_ref[0] * half_width, 128)
        for start, size in tiles_of(half_width):
            away_ref[:, start : start + size] = pull_back(
                offset + start, dpre, stat, w_ref, x_ref, gain_ref, scale_ref, size, full_width
            ).astype(jnp.bfloat16)

    return pl.pallas_call(
        body,
        in_specs=[SCALAR] + [WHOLE] * 7,
        out_specs=[WHOLE] * 4,
        out_shape=[
            jax.ShapeDtypeStruct((rows, half_width), jnp.bfloat16),
            jax.ShapeDtypeStruct((rows, 128), jnp.float32),
            jax.ShapeDtypeStruct((rows, half_width), jnp.bfloat16),
            pltpu.VMEM(weight.shape, weight.dtype),
        ],
        input_output_aliases={7: 3},
        compiler_params=pltpu.CompilerParams(vmem_limit_bytes=STEP_VMEM),
    )(core, upstream, slope, preact, inputs, row_scale, gain, in_vmem(weight))


def backward_home(core, upstream, dpre, stat, inputs, row_scale, gain, weight):
    rows, full_width = inputs.shape
    half_width = weight.shape[1]

    def body(core_ref, up_ref, dpre_ref, stat_ref, x_ref, scale_ref, gain_ref, w_ref, home_ref, _):
        dpre = dpre_ref[...]
        offset = pl.multiple_of(core_ref[0] * half_width, 128)
        for start, size in tiles_of(half_width):
            home_ref[:, start : start + size] = up_ref[:, start : start + size].astype(
                jnp.float32
            ) + pull_back(
                offset + start, dpre, stat_ref[:, :1], w_ref, x_ref, gain_ref, scale_ref, size, full_width
            )

    return pl.pallas_call(
        body,
        in_specs=[SCALAR] + [WHOLE] * 7,
        out_specs=[WHOLE, WHOLE],
        out_shape=[
            jax.ShapeDtypeStruct((rows, half_width), jnp.float32),
            pltpu.VMEM(weight.shape, weight.dtype),
        ],
        input_output_aliases={7: 1},
        compiler_params=pltpu.CompilerParams(vmem_limit_bytes=STEP_VMEM),
    )(core, upstream, dpre, stat, inputs, row_scale, gain, in_vmem(weight))


def adam(row_order, sides, features, dpre, master, moment_one, moment_two):
    blocks, rows, width = moment_one.shape
    depth = dpre.shape[0]
    strip = 16 if rows % 16 == 0 else rows
    fix_one = 1.0 - beta_one**step_count
    fix_two = 1.0 - beta_two**step_count

    def body(order_ref, side_ref, feature_ref, dpre_ref, w_ref, m_ref, *refs):
        second_refs, refs = refs[:blocks], refs[blocks:]
        new_w_ref, new_m_ref, new_v_ref, grad_ref, v_ref, sems = refs
        block = pl.program_id(0)

        def fetch(k):
            source = second_refs[k].at[side_ref[k]] if k else second_refs[k]
            return pltpu.make_async_copy(source, v_ref.at[k % 2], sems.at[k % 2])

        @pl.when(block == 0)
        def _():
            fetch(0).start()

        for k in range(blocks):

            @pl.when(block == k)
            def _(k=k):
                if k + 1 < blocks:
                    fetch(k + 1).start()
                fetch(k).wait()

        now = lax.rem(block, 2)
        grad_ref[...] = jnp.dot(
            feature_ref[0], dpre_ref[...], preferred_element_type=jnp.float32
        )

        def step(index, carry):
            part = pl.ds(index * strip, strip)
            grad = grad_ref[part, :]
            moment_next = beta_one * m_ref[0, part, :].astype(jnp.float32) + (1.0 - beta_one) * grad
            second_next = (
                beta_two * v_ref[now, part, :].astype(jnp.float32) + (1.0 - beta_two) * grad * grad
            )
            scaled = second_next / fix_two
            root = scaled * lax.rsqrt(scaled)
            direction = moment_next / fix_one * pl.reciprocal(root + adam_eps, approx=True)
            rows_w = w_ref[0, part, :].astype(jnp.float32)
            new_w_ref[0, part, :] = rows_w - learn_rate * (direction + decay_rate * rows_w)
            new_m_ref[0, part, :] = moment_next.astype(jnp.bfloat16)
            new_v_ref[0, part, :] = second_next.astype(jnp.bfloat16)
            return carry

        lax.fori_loop(0, rows // strip, step, 0)

    def placed(i, order_ref, side_ref):
        return (order_ref[i], 0, 0)

    tile = pl.BlockSpec((1, rows, width), placed)
    return pl.pallas_call(
        body,
        grid_spec=pltpu.PrefetchScalarGridSpec(
            num_scalar_prefetch=2,
            grid=(blocks,),
            in_specs=[
                pl.BlockSpec((1, rows, depth), placed),
                pl.BlockSpec((depth, width), lambda i, o, s: (0, 0)),
                tile,
                tile,
            ]
            + [pl.BlockSpec(memory_space=pl.ANY)] * blocks,
            out_specs=[tile, tile, tile],
            scratch_shapes=[
                pltpu.VMEM((rows, width), jnp.float32),
                pltpu.VMEM((2, rows, width), jnp.bfloat16),
                pltpu.SemaphoreType.DMA((2,)),
            ],
        ),
        out_shape=[
            jax.ShapeDtypeStruct((blocks, rows, width), jnp.float32),
            jax.ShapeDtypeStruct((blocks, rows, width), jnp.bfloat16),
            jax.ShapeDtypeStruct((blocks, rows, width), jnp.bfloat16),
        ],
        compiler_params=pltpu.CompilerParams(vmem_limit_bytes=ADAM_VMEM),
    )(
        row_order,
        sides,
        features,
        dpre,
        in_hbm(master),
        in_hbm(moment_one),
        *[in_hbm(piece) for piece in moment_two],
    )


def local(old_w, old_m, old_v, old_slot_layer, norm_gain, tokens, cotangent):
    sections = lax.axis_size("section")
    replicas = lax.axis_size("dp")
    cores = lax.axis_size("mp")
    section_index = lax.axis_index("section")
    replica_index = lax.axis_index("dp")
    core_index = lax.axis_index("mp")
    full_width = tokens.shape[2]
    half_width = old_w.shape[4]
    row_block = sections * old_w.shape[3]
    tokens = tokens.reshape(-1, full_width)
    cotangent = cotangent.reshape(-1, full_width)
    token_total = tokens.shape[0]
    group_rows = token_total // GROUPS
    layer_ids = jnp.arange(sections, dtype=jnp.int32)
    matches = (old_slot_layer[None, :] == layer_ids[:, None]).astype(jnp.int32)
    inverse = jnp.sum(matches * layer_ids[None, :], axis=1)
    own_w = relocate(ordered_copy(inverse, old_w))
    weight = lax.all_gather(own_w, "dp", axis=0, tiled=True)

    def meet(piece, by):
        groups = [[s, s ^ by] for s in range(sections) if s < s ^ by]
        return lax.all_gather(piece, "section", axis=0, tiled=False, axis_index_groups=groups)

    sources = section_index ^ layer_ids
    sides = (section_index < sources).astype(jnp.int32)
    picks = jnp.take(inverse, sources)
    early = picked_pieces(picks[:EARLY], old_v)
    received = [early[0]] + [meet(early[by], by) for by in range(1, EARLY)]
    picks_m = inverse + zero_after(own_w) + zero_after(received[-1])
    moment_one = relocate(ordered_copy(picks_m, old_m))
    late = picked_pieces(picks[EARLY:] + zero_after(own_w), old_v)
    received += [meet(late[by - EARLY], by) for by in range(EARLY, sections)]
    entry_section = section_index + zero_after(moment_one)
    weight = resident(weight)

    gain_row = norm_gain[0]

    def half_of(value, by=0):
        start = lax.rem(core_index + by, cores) * half_width
        return lax.dynamic_slice_in_dim(value, start, half_width, value.ndim - 1)

    def core_at(by):
        return lax.rem(core_index + by, cores).reshape(1)


    def put(stash, value, slot):
        return lax.dynamic_update_index_in_dim(stash, value, slot, 0)

    def get(stash, slot):
        return lax.dynamic_index_in_dim(stash, slot, 0, keepdims=False)

    def slot_of(group):
        return jnp.where((group >= 0) & (group < GROUPS), group, GROUPS)

    def hop(value, tick, by):
        senders = [tick - group for group in range(GROUPS) if 0 <= tick - group < sections - 1]
        pairs = [(s, s + 1) for s in senders]
        if by < 0:
            pairs = [(sections - 1 - s, sections - 2 - s) for s in senders]
        return lax.ppermute(value, "section", pairs)

    acts = jnp.zeros((GROUPS + 1, group_rows, full_width), jnp.bfloat16)
    norms = jnp.zeros((GROUPS + 1, group_rows, full_width), jnp.bfloat16)
    preacts = jnp.zeros((GROUPS + 1, group_rows, half_width), jnp.float32)
    slopes = jnp.zeros((GROUPS + 1, group_rows, half_width), jnp.float32)
    scales = jnp.zeros((GROUPS + 1, group_rows, 128), jnp.float32)
    dpres = jnp.zeros((GROUPS + 1, group_rows, half_width), jnp.bfloat16)
    ticks = GROUPS + sections - 1
    features = None
    forward_in = jnp.zeros((group_rows, full_width), jnp.bfloat16)
    backward_in = jnp.zeros((group_rows, half_width), jnp.bfloat16)

    def forward_tick(tick, arriving, stash, weight):
        acts, norms, preacts, slopes, scales = stash
        slot = slot_of(tick - section_index)
        inputs = arriving
        if tick < GROUPS:
            entry = tokens[tick * group_rows : (tick + 1) * group_rows]
            inputs = jnp.where(entry_section == 0, entry, arriving)
        output, normed, preact, scale, weight = forward_step(core_at(0), inputs, norm_gain, weight)
        sigmoid_value = jax.nn.sigmoid(preact)
        slope = sigmoid_value * (1.0 + preact * (1.0 - sigmoid_value))
        stash = (
            put(acts, inputs, slot),
            put(norms, normed, slot),
            put(preacts, preact, slot),
            put(slopes, slope, slot),
            put(scales, scale, slot),
        )
        if tick < ticks - 1:
            arriving = lax.all_gather(hop(output, tick, 1), "mp", axis=1, tiled=True)
        return arriving, stash, weight

    def backward_tick(tick, arriving, stash, dpres, weight):
        acts, _, preacts, slopes, scales = stash
        slot = slot_of(tick - (sections - 1 - section_index))
        slope, preact, inputs = get(slopes, slot), get(preacts, slot), get(acts, slot)
        row_scale = get(scales, slot)
        slope, preact, row_scale, inputs = lax.optimization_barrier(
            (slope, preact, row_scale, inputs)
        )
        upstream = arriving
        if tick < GROUPS:
            seed = cotangent[tick * group_rows : (tick + 1) * group_rows]
            upstream = jnp.where(section_index == sections - 1, half_of(seed), arriving)
        if tick == ticks - 1:
            dpre = (upstream.astype(jnp.float32) * slope).astype(jnp.bfloat16)
            return arriving, put(dpres, dpre, slot), weight
        for by in range(1, cores):
            dpre, stat, away, weight = backward_away(
                core_at(by), upstream, slope, preact, inputs, row_scale, norm_gain, weight
            )
            came = turn(away, "mp", by)
        home, weight = backward_home(
            core_at(0), upstream, dpre, stat, inputs, row_scale, norm_gain, weight
        )
        arriving = hop((home + came.astype(jnp.float32)).astype(jnp.bfloat16), tick, -1)
        return arriving, put(dpres, dpre, slot), weight

    stash = (acts, norms, preacts, slopes, scales)
    for tick in range(ticks - 1):
        forward_in, stash, weight = forward_tick(tick, forward_in, stash, weight)
    last_stash = stash
    for tick in range(ticks):
        if tick == 1:
            _, stash, weight = forward_tick(ticks - 1, forward_in, last_stash, weight)
        backward_in, dpres, weight = backward_tick(tick, backward_in, stash, dpres, weight)
        if tick == GROUPS:
            block_start = replica_index
            normed_all = stash[1][:GROUPS].reshape(token_total, full_width)
            features = []
            for by in range(replicas):
                block = lax.rem(block_start + by, replicas) * row_block
                part = lax.dynamic_slice_in_dim(normed_all, block, row_block, 1)
                features.append(turn(part, "dp", by) if by else part)
            features = jnp.concatenate(features, axis=0)
            features = features.T.reshape(sections, -1, replicas * token_total)

    dpre_all = dpres[:GROUPS].reshape(token_total, half_width)
    dpre_all = jnp.concatenate(
        [turn(dpre_all, "dp", by) if by else dpre_all for by in range(replicas)], axis=0
    )
    blocked = (sections, -1, half_width)
    updated = adam(
        sources,
        sides,
        features,
        dpre_all,
        own_w.reshape(blocked),
        moment_one.reshape(blocked),
        received,
    )
    return tuple(value.reshape(1, row_block, half_width) for value in updated)


def solution(mesh):
    placed = (
        P(None, "dp", "section", None, "mp"),
        P(None, "dp", "section", None, "mp"),
        P(None, "dp", "section", None, "mp"),
        P(),
        P("section", None),
        P(None, "dp", None),
        P(None, "dp", None),
    )
    return jax.shard_map(
        local,
        mesh=mesh,
        in_specs=placed,
        out_specs=(P("section", "dp", "mp"), P("section", "dp", "mp"), P("section", "dp", "mp")),
        check_vma=False,
    )
```

```python
import jax
import jax.numpy as jnp
from jax import lax
from jax.experimental import pallas as pl
from jax.experimental.pallas import tpu as pltpu
from jax.sharding import PartitionSpec as P

eps_norm = 1e-05
beta_one = 0.9
beta_two = 0.95
learn_rate = 0.001
decay_rate = 0.1
adam_eps = 1e-08
step_count = 1000.0

GROUPS = 2

FIRST_PART = 8
PARTS = 2
STEP_VMEM = 16 * 1024 * 1024
ADAM_VMEM = 24 * 1024 * 1024


def turn(value, axis, by):
    count = lax.axis_size(axis)
    return lax.ppermute(value, axis, [(i, (i + by) % count) for i in range(count)])


def zero_after(value):
    first = lax.slice(value, (0,) * value.ndim, (1,) * value.ndim).reshape(())
    return jnp.minimum((first > 0).astype(jnp.int32), 0)


def relocate(pieces):
    moved = lax.all_to_all(pieces, "section", split_axis=0, concat_axis=2, tiled=True)
    return moved.reshape(-1, moved.shape[-1])


def ordered_cast(picks, pieces, cuts):
    slots, _, _, rows, width = pieces.shape

    def body(pick_ref, in_ref, *out_refs):
        for (lo, hi), out_ref in zip(cuts, out_refs):
            out_ref[...] = in_ref[:, :, :, :, lo:hi].astype(out_ref.dtype)

    return pl.pallas_call(
        body,
        out_shape=[
            jax.ShapeDtypeStruct((slots, 1, 1, rows, hi - lo), jnp.bfloat16) for lo, hi in cuts
        ],
        grid_spec=pltpu.PrefetchScalarGridSpec(
            num_scalar_prefetch=1,
            grid=(slots,),
            in_specs=[pl.BlockSpec((1, 1, 1, rows, width), lambda i, p: (p[i], 0, 0, 0, 0))],
            out_specs=[
                pl.BlockSpec((1, 1, 1, rows, hi - lo), lambda i, p: (i, 0, 0, 0, 0))
                for lo, hi in cuts
            ],
        ),
        compiler_params=pltpu.CompilerParams(vmem_limit_bytes=STEP_VMEM),
    )(picks, pieces)


def picked(picks, carry, sources, edges, stacked):
    rows = sources[0][0].shape[3]
    count = picks.shape[0]
    ends = [0]
    for _, lo, hi in sources:
        ends.append(ends[-1] + hi - lo)
    dtype = sources[0][0].dtype
    spans = list(zip(edges[:-1], edges[1:]))

    def body(pick_ref, carry_ref, *refs):
        in_refs, refs = refs[: len(sources)], refs[len(sources) :]
        carried_ref, out_refs, (held_ref, sems, out_sems) = refs[0], refs[1:-3], refs[-3:]
        incoming = [
            [
                pltpu.make_async_copy(
                    in_ref.at[pick_ref[i], 0, 0, :, lo:hi],
                    held_ref.at[i, :, ends[j] : ends[j + 1]],
                    sems.at[i, j],
                )
                for j, (in_ref, (_, lo, hi)) in enumerate(zip(in_refs, sources))
            ]
            for i in range(count)
        ]
        outgoing = [
            [
                pltpu.make_async_copy(
                    held_ref.at[i, :, lo:hi],
                    out_refs[0].at[i, 0, 0] if stacked else out_refs[i * len(spans) + j],
                    out_sems.at[i, j],
                )
                for j, (lo, hi) in enumerate(spans)
            ]
            for i in range(count)
        ]
        for copies in incoming:
            for copy in copies:
                copy.start()
        for i in range(carry_ref.shape[0]):
            carried_ref[i] = carry_ref[i]
        for arrive, leave in zip(incoming, outgoing):
            for copy in arrive:
                copy.wait()
            for copy in leave:
                copy.start()
        for copies in outgoing:
            for copy in copies:
                copy.wait()

    if stacked:
        shapes = [jax.ShapeDtypeStruct((count, 1, 1, rows, ends[-1]), dtype)]
    else:
        shapes = [jax.ShapeDtypeStruct((rows, hi - lo), dtype) for lo, hi in spans] * count
    carried, *pieces = pl.pallas_call(
        body,
        out_shape=[jax.ShapeDtypeStruct(carry.shape, carry.dtype)] + shapes,
        in_specs=[SCALAR, SCALAR] + [ANYWHERE] * len(sources),
        out_specs=[SCALAR] + [ANYWHERE] * len(shapes),
        scratch_shapes=[
            pltpu.VMEM((count, rows, ends[-1]), dtype),
            pltpu.SemaphoreType.DMA((count, len(sources))),
            pltpu.SemaphoreType.DMA((count, len(spans))),
        ],
        compiler_params=pltpu.CompilerParams(vmem_limit_bytes=STEP_VMEM),
    )(picks, carry, *[in_hbm(array) for array, _, _ in sources])
    if stacked:
        return carried, pieces[0]
    return carried, [pieces[i * len(spans) : (i + 1) * len(spans)] for i in range(count)]


def resident(replica, blocks, cuts):
    replicas = len(blocks)
    rows = blocks[0][0].shape[0]
    flat = [piece for line in blocks for piece in line]

    def body(replica_ref, *refs):
        piece_refs, out_ref, sems = refs[:-2], refs[-2], refs[-1]
        copies = []
        for index, piece_ref in enumerate(piece_refs):
            by, (lo, hi) = index // len(cuts), cuts[index % len(cuts)]
            owner = lax.rem(replica_ref[0] + replicas - by, replicas)
            start = pl.multiple_of(owner * rows, 16)
            copies.append(
                pltpu.make_async_copy(
                    piece_ref, out_ref.at[pl.ds(start, rows), lo:hi], sems.at[index]
                )
            )
        for copy in copies:
            copy.start()
        for copy in copies:
            copy.wait()

    return pl.pallas_call(
        body,
        out_shape=pltpu.VMEM((replicas * rows, cuts[-1][1]), flat[0].dtype),
        in_specs=[SCALAR] + [ANYWHERE] * len(flat),
        out_specs=pl.BlockSpec(memory_space=pltpu.VMEM),
        scratch_shapes=[pltpu.SemaphoreType.DMA((len(flat),))],
        compiler_params=pltpu.CompilerParams(vmem_limit_bytes=STEP_VMEM),
    )(replica, *[in_hbm(piece) for piece in flat])


def tiles_of(width):
    return [(start, min(256, width - start)) for start in range(0, width, 256)]


def in_vmem(array):
    return pltpu.with_memory_space_constraint(array, pltpu.VMEM)


def in_hbm(array):
    return pltpu.with_memory_space_constraint(array, pltpu.HBM)


WHOLE = pl.BlockSpec(memory_space=pltpu.VMEM)
SCALAR = pl.BlockSpec(memory_space=pltpu.SMEM)
ANYWHERE = pl.BlockSpec(memory_space=pl.ANY)


def forward_step(core, inputs, gain, weight):
    rows, full_width = inputs.shape
    half_width = weight.shape[1]

    def body(core_ref, x_ref, gain_ref, w_ref, out_ref, normed_ref, preact_ref, scale_ref, _):
        wide = x_ref[...].astype(jnp.float32)
        scale = lax.rsqrt(jnp.mean(wide * wide, axis=1, keepdims=True) + eps_norm)
        normed = (wide * scale * gain_ref[...]).astype(jnp.bfloat16)
        normed_ref[...] = normed
        scale_ref[...] = jnp.broadcast_to(scale, scale_ref.shape)
        offset = pl.multiple_of(core_ref[0] * half_width, 128)
        for start, size in tiles_of(half_width):
            preact = jnp.dot(
                normed, w_ref[:, start : start + size], preferred_element_type=jnp.float32
            )
            preact_ref[:, start : start + size] = preact
            own = x_ref[:, pl.ds(pl.multiple_of(offset + start, 128), size)].astype(jnp.float32)
            silu = preact / (1.0 + jnp.exp(-preact))
            out_ref[:, start : start + size] = (own + silu).astype(jnp.bfloat16)

    return pl.pallas_call(
        body,
        in_specs=[SCALAR, WHOLE, WHOLE, WHOLE],
        out_specs=[WHOLE] * 5,
        out_shape=[
            jax.ShapeDtypeStruct((rows, half_width), jnp.bfloat16),
            jax.ShapeDtypeStruct((rows, full_width), jnp.bfloat16),
            jax.ShapeDtypeStruct((rows, half_width), jnp.float32),
            jax.ShapeDtypeStruct((rows, 128), jnp.float32),
            pltpu.VMEM(weight.shape, weight.dtype),
        ],
        input_output_aliases={3: 4},
        compiler_params=pltpu.CompilerParams(vmem_limit_bytes=STEP_VMEM),
    )(core, inputs, gain, in_vmem(weight))


def pull_back(start, dpre, stat, w_ref, x_ref, gain_ref, scale_ref, size, width):
    cols = pl.ds(pl.multiple_of(start, 128), size)
    product = lax.dot_general(
        dpre, w_ref[cols, :], (((1,), (1,)), ((), ())), preferred_element_type=jnp.float32
    )
    scale = scale_ref[:, :1]
    return scale * (
        gain_ref[:, cols] * product - x_ref[:, cols].astype(jnp.float32) * (scale * stat / width)
    )


def backward_away(core, upstream, slope, preact, inputs, row_scale, gain, weight):
    rows, full_width = inputs.shape
    half_width = weight.shape[1]

    def body(
        core_ref, up_ref, slope_ref, preact_ref, x_ref, scale_ref, gain_ref, w_ref,
        dpre_ref, stat_ref, away_ref, _,
    ):
        dpre = (up_ref[...].astype(jnp.float32) * slope_ref[...]).astype(jnp.bfloat16)
        dpre_ref[...] = dpre
        stat = jnp.sum(dpre.astype(jnp.float32) * preact_ref[...], axis=1, keepdims=True)
        stat_ref[...] = jnp.broadcast_to(stat, stat_ref.shape)
        offset = pl.multiple_of(core_ref[0] * half_width, 128)
        for start, size in tiles_of(half_width):
            away_ref[:, start : start + size] = pull_back(
                offset + start, dpre, stat, w_ref, x_ref, gain_ref, scale_ref, size, full_width
            ).astype(jnp.bfloat16)

    return pl.pallas_call(
        body,
        in_specs=[SCALAR] + [WHOLE] * 7,
        out_specs=[WHOLE] * 4,
        out_shape=[
            jax.ShapeDtypeStruct((rows, half_width), jnp.bfloat16),
            jax.ShapeDtypeStruct((rows, 128), jnp.float32),
            jax.ShapeDtypeStruct((rows, half_width), jnp.bfloat16),
            pltpu.VMEM(weight.shape, weight.dtype),
        ],
        input_output_aliases={7: 3},
        compiler_params=pltpu.CompilerParams(vmem_limit_bytes=STEP_VMEM),
    )(core, upstream, slope, preact, inputs, row_scale, gain, in_vmem(weight))


def backward_home(core, upstream, dpre, stat, inputs, row_scale, gain, weight):
    rows, full_width = inputs.shape
    half_width = weight.shape[1]

    def body(core_ref, up_ref, dpre_ref, stat_ref, x_ref, scale_ref, gain_ref, w_ref, home_ref, _):
        dpre = dpre_ref[...]
        offset = pl.multiple_of(core_ref[0] * half_width, 128)
        for start, size in tiles_of(half_width):
            home_ref[:, start : start + size] = up_ref[:, start : start + size].astype(
                jnp.float32
            ) + pull_back(
                offset + start, dpre, stat_ref[:, :1], w_ref, x_ref, gain_ref, scale_ref, size, full_width
            )

    return pl.pallas_call(
        body,
        in_specs=[SCALAR] + [WHOLE] * 7,
        out_specs=[WHOLE, WHOLE],
        out_shape=[
            jax.ShapeDtypeStruct((rows, half_width), jnp.float32),
            pltpu.VMEM(weight.shape, weight.dtype),
        ],
        input_output_aliases={7: 1},
        compiler_params=pltpu.CompilerParams(vmem_limit_bytes=STEP_VMEM),
    )(core, upstream, dpre, stat, inputs, row_scale, gain, in_vmem(weight))


def adam(row_order, sides, features, dpre, masters, moment_one, moments, cuts):
    blocks, rows, first_width = moment_one.shape
    depth, width = dpre.shape
    parts = len(moments[0])
    strip = 16 if rows % 16 == 0 else rows
    fix_one = 1.0 - beta_one**step_count
    fix_two = 1.0 - beta_two**step_count

    def body(order_ref, side_ref, feature_ref, dpre_ref, *refs):
        w_refs, m_ref, refs = refs[: len(cuts)], refs[len(cuts)], refs[len(cuts) + 1 :]
        piece_refs, refs = refs[: blocks * parts], refs[blocks * parts :]
        new_w_ref, new_m_ref, new_v_ref, grad_ref, held_ref, sems = refs
        block = pl.program_id(0)

        def fetch(k):
            copies, start = [], 0
            for which in range(parts):
                piece = piece_refs[parts * k + which]
                piece = piece.at[side_ref[k]] if k else piece
                end = start + piece.shape[-1]
                copies.append(
                    pltpu.make_async_copy(
                        piece, held_ref.at[k % 2, :, start:end], sems.at[which, k % 2]
                    )
                )
                start = end
            return copies

        @pl.when(block == 0)
        def _():
            for copy in fetch(0):
                copy.start()

        for k in range(blocks):

            @pl.when(block == k)
            def _(k=k):
                if k + 1 < blocks:
                    for copy in fetch(k + 1):
                        copy.start()

        grad_ref[...] = jnp.dot(feature_ref[0], dpre_ref[...], preferred_element_type=jnp.float32)

        for k in range(blocks):

            @pl.when(block == k)
            def _(k=k):
                for copy in fetch(k):
                    copy.wait()

        now = lax.rem(block, 2)

        def step(index, carry):
            part = pl.ds(index * strip, strip)
            for which, (lo, hi) in enumerate(cuts):
                grad = grad_ref[part, lo:hi]
                first = held_ref[now, part, width:] if which else m_ref[0, part, :]
                moment_next = beta_one * first.astype(jnp.float32) + (1.0 - beta_one) * grad
                second_next = (
                    beta_two * held_ref[now, part, lo:hi].astype(jnp.float32)
                    + (1.0 - beta_two) * grad * grad
                )
                scaled = second_next / fix_two
                root = scaled * lax.rsqrt(scaled)
                direction = moment_next / fix_one * pl.reciprocal(root + adam_eps, approx=True)
                rows_w = w_refs[which][0, part, :].astype(jnp.float32)
                new_w_ref[0, part, lo:hi] = rows_w - learn_rate * (direction + decay_rate * rows_w)
                new_m_ref[0, part, lo:hi] = moment_next.astype(jnp.bfloat16)
                new_v_ref[0, part, lo:hi] = second_next.astype(jnp.bfloat16)
            return carry

        lax.fori_loop(0, rows // strip, step, 0)

    def placed(i, order_ref, side_ref):
        return (order_ref[i], 0, 0)

    tile = pl.BlockSpec((1, rows, width), placed)
    return pl.pallas_call(
        body,
        grid_spec=pltpu.PrefetchScalarGridSpec(
            num_scalar_prefetch=2,
            grid=(blocks,),
            in_specs=[
                pl.BlockSpec((1, rows, depth), placed),
                pl.BlockSpec((depth, width), lambda i, o, s: (0, 0)),
            ]
            + [pl.BlockSpec((1, rows, hi - lo), placed) for lo, hi in cuts]
            + [pl.BlockSpec((1, rows, first_width), placed)]
            + [ANYWHERE] * (blocks * parts),
            out_specs=[tile, tile, tile],
            scratch_shapes=[
                pltpu.VMEM((rows, width), jnp.float32),
                pltpu.VMEM((2, rows, 2 * width - first_width), jnp.bfloat16),
                pltpu.SemaphoreType.DMA((parts, 2)),
            ],
        ),
        out_shape=[
            jax.ShapeDtypeStruct((blocks, rows, width), jnp.float32),
            jax.ShapeDtypeStruct((blocks, rows, width), jnp.bfloat16),
            jax.ShapeDtypeStruct((blocks, rows, width), jnp.bfloat16),
        ],
        compiler_params=pltpu.CompilerParams(vmem_limit_bytes=ADAM_VMEM),
    )(
        row_order,
        sides,
        features,
        dpre,
        *[in_hbm(piece) for piece in masters],
        in_hbm(moment_one),
        *[in_hbm(piece) for pieces in moments for piece in pieces],
    )


def local(old_w, old_m, old_v, old_slot_layer, norm_gain, tokens, cotangent):
    sections = lax.axis_size("section")
    replicas = lax.axis_size("dp")
    cores = lax.axis_size("mp")
    section_index = lax.axis_index("section")
    replica_index = lax.axis_index("dp")
    core_index = lax.axis_index("mp")
    full_width = tokens.shape[2]
    half_width = old_w.shape[4]
    row_block = sections * old_w.shape[3]
    tokens = tokens.reshape(-1, full_width)
    cotangent = cotangent.reshape(-1, full_width)
    token_total = tokens.shape[0]
    group_rows = token_total // GROUPS
    layer_ids = jnp.arange(sections, dtype=jnp.int32)
    matches = (old_slot_layer[None, :] == layer_ids[:, None]).astype(jnp.int32)
    inverse = jnp.sum(matches * layer_ids[None, :], axis=1)
    lanes = half_width // 128
    middle = lanes * FIRST_PART // 16 * 128
    cuts = [(0, middle), (middle, half_width)]
    sources = section_index ^ layer_ids
    sides = (section_index < sources).astype(jnp.int32)
    picks = jnp.take(inverse, sources)
    early = sections // 2
    breadth = 2 * half_width - middle
    edges = [breadth // 128 * part // PARTS * 128 for part in range(PARTS)] + [breadth]
    travelling = [(old_v, 0, half_width), (old_m, middle, half_width)]
    carried, sent = picked(picks[:early], inverse, travelling, edges, False)
    own_w = [relocate(piece) for piece in ordered_cast(carried, old_w, cuts)]
    blocks = [
        [turn(piece, "dp", by) if by else piece for piece in own_w] for by in range(replicas)
    ]

    def meet(piece, by):
        groups = [[s, s ^ by] for s in range(sections) if s < s ^ by]
        return lax.all_gather(piece, "section", axis=0, tiled=False, axis_index_groups=groups)

    moments = [sent[0]] + [[meet(piece, by) for piece in sent[by]] for by in range(1, early)]
    held = zero_after(blocks[-1][-1])
    _, ordered_m = picked(inverse + held, inverse, [(old_m, 0, middle)], [0, middle], True)
    moment_one = relocate(ordered_m)
    later = picks[early:] + zero_after(own_w[-1])
    _, sent = picked(later, inverse, travelling, edges, False)
    moments += [[meet(piece, by) for piece in sent[by - early]] for by in range(early, sections)]
    entry_section = section_index
    weight = resident((replica_index + zero_after(moment_one)).reshape(1), blocks, cuts)

    gain_row = norm_gain[0]

    def half_of(value, by=0):
        start = lax.rem(core_index + by, cores) * half_width
        return lax.dynamic_slice_in_dim(value, start, half_width, value.ndim - 1)

    def core_at(by):
        return lax.rem(core_index + by, cores).reshape(1)


    def put(stash, value, slot):
        return lax.dynamic_update_index_in_dim(stash, value, slot, 0)

    def get(stash, slot):
        return lax.dynamic_index_in_dim(stash, slot, 0, keepdims=False)

    def slot_of(group):
        return jnp.where((group >= 0) & (group < GROUPS), group, GROUPS)

    def hop(value, tick, by):
        senders = [tick - group for group in range(GROUPS) if 0 <= tick - group < sections - 1]
        pairs = [(s, s + 1) for s in senders]
        if by < 0:
            pairs = [(sections - 1 - s, sections - 2 - s) for s in senders]
        return lax.ppermute(value, "section", pairs)

    acts = jnp.zeros((GROUPS + 1, group_rows, full_width), jnp.bfloat16)
    norms = jnp.zeros((GROUPS + 1, group_rows, full_width), jnp.bfloat16)
    preacts = jnp.zeros((GROUPS + 1, group_rows, half_width), jnp.float32)
    slopes = jnp.zeros((GROUPS + 1, group_rows, half_width), jnp.float32)
    scales = jnp.zeros((GROUPS + 1, group_rows, 128), jnp.float32)
    dpres = jnp.zeros((GROUPS + 1, group_rows, half_width), jnp.bfloat16)
    ticks = GROUPS + sections - 1
    features = None
    forward_in = jnp.zeros((group_rows, full_width), jnp.bfloat16)
    backward_in = jnp.zeros((group_rows, half_width), jnp.bfloat16)

    def forward_tick(tick, arriving, stash, weight):
        acts, norms, preacts, slopes, scales = stash
        slot = slot_of(tick - section_index)
        inputs = arriving
        if tick < GROUPS:
            entry = tokens[tick * group_rows : (tick + 1) * group_rows]
            inputs = jnp.where(entry_section == 0, entry, arriving)
        output, normed, preact, scale, weight = forward_step(core_at(0), inputs, norm_gain, weight)
        sigmoid_value = jax.nn.sigmoid(preact)
        slope = sigmoid_value * (1.0 + preact * (1.0 - sigmoid_value))
        stash = (
            put(acts, inputs, slot),
            put(norms, normed, slot),
            put(preacts, preact, slot),
            put(slopes, slope, slot),
            put(scales, scale, slot),
        )
        if tick < ticks - 1:
            arriving = lax.all_gather(hop(output, tick, 1), "mp", axis=1, tiled=True)
        return arriving, stash, weight

    def backward_tick(tick, arriving, stash, dpres, weight):
        acts, _, preacts, slopes, scales = stash
        slot = slot_of(tick - (sections - 1 - section_index))
        slope, preact, inputs = get(slopes, slot), get(preacts, slot), get(acts, slot)
        row_scale = get(scales, slot)
        slope, preact, row_scale, inputs = lax.optimization_barrier(
            (slope, preact, row_scale, inputs)
        )
        upstream = arriving
        if tick < GROUPS:
            seed = cotangent[tick * group_rows : (tick + 1) * group_rows]
            upstream = jnp.where(section_index == sections - 1, half_of(seed), arriving)
        if tick == ticks - 1:
            dpre = (upstream.astype(jnp.float32) * slope).astype(jnp.bfloat16)
            return arriving, put(dpres, dpre, slot), weight
        for by in range(1, cores):
            dpre, stat, away, weight = backward_away(
                core_at(by), upstream, slope, preact, inputs, row_scale, norm_gain, weight
            )
            came = turn(away, "mp", by)
        home, weight = backward_home(
            core_at(0), upstream, dpre, stat, inputs, row_scale, norm_gain, weight
        )
        arriving = hop((home + came.astype(jnp.float32)).astype(jnp.bfloat16), tick, -1)
        return arriving, put(dpres, dpre, slot), weight

    stash = (acts, norms, preacts, slopes, scales)
    for tick in range(ticks - 1):
        forward_in, stash, weight = forward_tick(tick, forward_in, stash, weight)
    last_stash = stash
    for tick in range(ticks):
        if tick == 1:
            _, stash, weight = forward_tick(ticks - 1, forward_in, last_stash, weight)
        backward_in, dpres, weight = backward_tick(tick, backward_in, stash, dpres, weight)
        if tick == ticks - 2:
            settled = dpres[: GROUPS - 1].reshape(-1, half_width)
        if tick == GROUPS:
            block_start = replica_index
            normed_all = stash[1][:GROUPS].reshape(token_total, full_width)
            features = []
            for by in range(replicas):
                block = lax.rem(block_start + by, replicas) * row_block
                part = lax.dynamic_slice_in_dim(normed_all, block, row_block, 1)
                features.append(turn(part, "dp", by) if by else part)
            features = jnp.concatenate(features, axis=0)
            features = features.T.reshape(sections, -1, replicas * token_total)

    gathered = []
    for by in range(replicas):
        for part in (settled, dpres[GROUPS - 1]):
            gathered.append(turn(part, "dp", by) if by else part)
    blocked = (sections, -1)
    updated = adam(
        sources,
        sides,
        features,
        jnp.concatenate(gathered, axis=0),
        [piece.reshape(blocked + piece.shape[1:]) for piece in own_w],
        moment_one.reshape(blocked + moment_one.shape[1:]),
        moments,
        cuts,
    )
    return tuple(value.reshape(1, row_block, half_width) for value in updated)


def solution(mesh):
    placed = (
        P(None, "dp", "section", None, "mp"),
        P(None, "dp", "section", None, "mp"),
        P(None, "dp", "section", None, "mp"),
        P(),
        P("section", None),
        P(None, "dp", None),
        P(None, "dp", None),
    )
    return jax.shard_map(
        local,
        mesh=mesh,
        in_specs=placed,
        out_specs=(P("section", "dp", "mp"), P("section", "dp", "mp"), P("section", "dp", "mp")),
        check_vma=False,
    )
```

```python
import jax
import jax.numpy as jnp
from jax import lax
from jax.experimental import pallas as pl
from jax.experimental.pallas import tpu as pltpu
from jax.sharding import PartitionSpec as P

eps_norm = 1e-05
beta_one = 0.9
beta_two = 0.95
learn_rate = 0.001
decay_rate = 0.1
adam_eps = 1e-08
step_count = 1000.0

GROUPS = 2

FIRST_PART = 8
PARTS = 2
STEP_VMEM = 16 * 1024 * 1024
ADAM_VMEM = 24 * 1024 * 1024


def turn(value, axis, by):
    count = lax.axis_size(axis)
    return lax.ppermute(value, axis, [(i, (i + by) % count) for i in range(count)])


def zero_after(value):
    first = lax.slice(value, (0,) * value.ndim, (1,) * value.ndim).reshape(())
    return jnp.minimum((first > 0).astype(jnp.int32), 0)


def relocate(pieces):
    moved = lax.all_to_all(pieces, "section", split_axis=0, concat_axis=2, tiled=True)
    return moved.reshape(-1, moved.shape[-1])


def ordered_cast(picks, pieces, cuts):
    slots, _, _, rows, width = pieces.shape

    def body(pick_ref, in_ref, *out_refs):
        for (lo, hi), out_ref in zip(cuts, out_refs):
            out_ref[...] = in_ref[:, :, :, :, lo:hi].astype(out_ref.dtype)

    return pl.pallas_call(
        body,
        out_shape=[
            jax.ShapeDtypeStruct((slots, 1, 1, rows, hi - lo), jnp.bfloat16) for lo, hi in cuts
        ],
        grid_spec=pltpu.PrefetchScalarGridSpec(
            num_scalar_prefetch=1,
            grid=(slots,),
            in_specs=[pl.BlockSpec((1, 1, 1, rows, width), lambda i, p: (p[i], 0, 0, 0, 0))],
            out_specs=[
                pl.BlockSpec((1, 1, 1, rows, hi - lo), lambda i, p: (i, 0, 0, 0, 0))
                for lo, hi in cuts
            ],
        ),
        compiler_params=pltpu.CompilerParams(vmem_limit_bytes=STEP_VMEM),
    )(picks, pieces)


def picked(picks, carry, sources, edges, stacked):
    rows = sources[0][0].shape[3]
    count = picks.shape[0]
    ends = [0]
    for _, lo, hi in sources:
        ends.append(ends[-1] + hi - lo)
    dtype = sources[0][0].dtype
    spans = list(zip(edges[:-1], edges[1:]))

    def body(pick_ref, carry_ref, *refs):
        in_refs, refs = refs[: len(sources)], refs[len(sources) :]
        carried_ref, out_refs, (held_ref, sems, out_sems) = refs[0], refs[1:-3], refs[-3:]
        incoming = [
            [
                pltpu.make_async_copy(
                    in_ref.at[pick_ref[i], 0, 0, :, lo:hi],
                    held_ref.at[i, :, ends[j] : ends[j + 1]],
                    sems.at[i, j],
                )
                for j, (in_ref, (_, lo, hi)) in enumerate(zip(in_refs, sources))
            ]
            for i in range(count)
        ]
        outgoing = [
            [
                pltpu.make_async_copy(
                    held_ref.at[i, :, lo:hi],
                    out_refs[0].at[i, 0, 0] if stacked else out_refs[i * len(spans) + j],
                    out_sems.at[i, j],
                )
                for j, (lo, hi) in enumerate(spans)
            ]
            for i in range(count)
        ]
        for copies in incoming:
            for copy in copies:
                copy.start()
        for i in range(carry_ref.shape[0]):
            carried_ref[i] = carry_ref[i]
        for arrive, leave in zip(incoming, outgoing):
            for copy in arrive:
                copy.wait()
            for copy in leave:
                copy.start()
        for copies in outgoing:
            for copy in copies:
                copy.wait()

    if stacked:
        shapes = [jax.ShapeDtypeStruct((count, 1, 1, rows, ends[-1]), dtype)]
    else:
        shapes = [jax.ShapeDtypeStruct((rows, hi - lo), dtype) for lo, hi in spans] * count
    carried, *pieces = pl.pallas_call(
        body,
        out_shape=[jax.ShapeDtypeStruct(carry.shape, carry.dtype)] + shapes,
        in_specs=[SCALAR, SCALAR] + [ANYWHERE] * len(sources),
        out_specs=[SCALAR] + [ANYWHERE] * len(shapes),
        scratch_shapes=[
            pltpu.VMEM((count, rows, ends[-1]), dtype),
            pltpu.SemaphoreType.DMA((count, len(sources))),
            pltpu.SemaphoreType.DMA((count, len(spans))),
        ],
        compiler_params=pltpu.CompilerParams(vmem_limit_bytes=STEP_VMEM),
    )(picks, carry, *[in_hbm(array) for array, _, _ in sources])
    if stacked:
        return carried, pieces[0]
    return carried, [pieces[i * len(spans) : (i + 1) * len(spans)] for i in range(count)]


def resident(replica, blocks, cuts):
    replicas = len(blocks)
    rows = blocks[0][0].shape[0]
    flat = [piece for line in blocks for piece in line]

    def body(replica_ref, *refs):
        piece_refs, out_ref, sems = refs[:-2], refs[-2], refs[-1]
        copies = []
        for index, piece_ref in enumerate(piece_refs):
            by, (lo, hi) = index // len(cuts), cuts[index % len(cuts)]
            owner = lax.rem(replica_ref[0] + replicas - by, replicas)
            start = pl.multiple_of(owner * rows, 16)
            copies.append(
                pltpu.make_async_copy(
                    piece_ref, out_ref.at[pl.ds(start, rows), lo:hi], sems.at[index]
                )
            )
        for copy in copies:
            copy.start()
        for copy in copies:
            copy.wait()

    return pl.pallas_call(
        body,
        out_shape=pltpu.VMEM((replicas * rows, cuts[-1][1]), flat[0].dtype),
        in_specs=[SCALAR] + [ANYWHERE] * len(flat),
        out_specs=pl.BlockSpec(memory_space=pltpu.VMEM),
        scratch_shapes=[pltpu.SemaphoreType.DMA((len(flat),))],
        compiler_params=pltpu.CompilerParams(vmem_limit_bytes=STEP_VMEM),
    )(replica, *[in_hbm(piece) for piece in flat])


def tiles_of(width):
    return [(start, min(256, width - start)) for start in range(0, width, 256)]


def in_vmem(array):
    return pltpu.with_memory_space_constraint(array, pltpu.VMEM)


def in_hbm(array):
    return pltpu.with_memory_space_constraint(array, pltpu.HBM)


WHOLE = pl.BlockSpec(memory_space=pltpu.VMEM)
SCALAR = pl.BlockSpec(memory_space=pltpu.SMEM)
ANYWHERE = pl.BlockSpec(memory_space=pl.ANY)


def forward_step(core, inputs, gain, weight):
    rows, full_width = inputs.shape
    half_width = weight.shape[1]

    def body(core_ref, x_ref, gain_ref, w_ref, out_ref, normed_ref, preact_ref, scale_ref, _):
        wide = x_ref[...].astype(jnp.float32)
        scale = lax.rsqrt(jnp.mean(wide * wide, axis=1, keepdims=True) + eps_norm)
        normed = (wide * scale * gain_ref[...]).astype(jnp.bfloat16)
        normed_ref[...] = normed
        scale_ref[...] = jnp.broadcast_to(scale, scale_ref.shape)
        offset = pl.multiple_of(core_ref[0] * half_width, 128)
        for start, size in tiles_of(half_width):
            preact = jnp.dot(
                normed, w_ref[:, start : start + size], preferred_element_type=jnp.float32
            )
            preact_ref[:, start : start + size] = preact
            own = x_ref[:, pl.ds(pl.multiple_of(offset + start, 128), size)].astype(jnp.float32)
            silu = preact / (1.0 + jnp.exp(-preact))
            out_ref[:, start : start + size] = (own + silu).astype(jnp.bfloat16)

    return pl.pallas_call(
        body,
        in_specs=[SCALAR, WHOLE, WHOLE, WHOLE],
        out_specs=[WHOLE] * 5,
        out_shape=[
            jax.ShapeDtypeStruct((rows, half_width), jnp.bfloat16),
            jax.ShapeDtypeStruct((rows, full_width), jnp.bfloat16),
            jax.ShapeDtypeStruct((rows, half_width), jnp.float32),
            jax.ShapeDtypeStruct((rows, 128), jnp.float32),
            pltpu.VMEM(weight.shape, weight.dtype),
        ],
        input_output_aliases={3: 4},
        compiler_params=pltpu.CompilerParams(vmem_limit_bytes=STEP_VMEM),
    )(core, inputs, gain, in_vmem(weight))


def pull_back(start, dpre, stat, w_ref, x_ref, gain_ref, scale_ref, size, width):
    cols = pl.ds(pl.multiple_of(start, 128), size)
    product = lax.dot_general(
        dpre, w_ref[cols, :], (((1,), (1,)), ((), ())), preferred_element_type=jnp.float32
    )
    scale = scale_ref[:, :1]
    return scale * (
        gain_ref[:, cols] * product - x_ref[:, cols].astype(jnp.float32) * (scale * stat / width)
    )


def backward_away(core, upstream, slope, preact, inputs, row_scale, gain, weight):
    rows, full_width = inputs.shape
    half_width = weight.shape[1]

    def body(
        core_ref, up_ref, slope_ref, preact_ref, x_ref, scale_ref, gain_ref, w_ref,
        dpre_ref, stat_ref, away_ref, _,
    ):
        dpre = (up_ref[...].astype(jnp.float32) * slope_ref[...]).astype(jnp.bfloat16)
        dpre_ref[...] = dpre
        stat = jnp.sum(dpre.astype(jnp.float32) * preact_ref[...], axis=1, keepdims=True)
        stat_ref[...] = jnp.broadcast_to(stat, stat_ref.shape)
        offset = pl.multiple_of(core_ref[0] * half_width, 128)
        for start, size in tiles_of(half_width):
            away_ref[:, start : start + size] = pull_back(
                offset + start, dpre, stat, w_ref, x_ref, gain_ref, scale_ref, size, full_width
            ).astype(jnp.bfloat16)

    return pl.pallas_call(
        body,
        in_specs=[SCALAR] + [WHOLE] * 7,
        out_specs=[WHOLE] * 4,
        out_shape=[
            jax.ShapeDtypeStruct((rows, half_width), jnp.bfloat16),
            jax.ShapeDtypeStruct((rows, 128), jnp.float32),
            jax.ShapeDtypeStruct((rows, half_width), jnp.bfloat16),
            pltpu.VMEM(weight.shape, weight.dtype),
        ],
        input_output_aliases={7: 3},
        compiler_params=pltpu.CompilerParams(vmem_limit_bytes=STEP_VMEM),
    )(core, upstream, slope, preact, inputs, row_scale, gain, in_vmem(weight))


def backward_home(core, upstream, dpre, stat, inputs, row_scale, gain, weight):
    rows, full_width = inputs.shape
    half_width = weight.shape[1]

    def body(core_ref, up_ref, dpre_ref, stat_ref, x_ref, scale_ref, gain_ref, w_ref, home_ref, _):
        dpre = dpre_ref[...]
        offset = pl.multiple_of(core_ref[0] * half_width, 128)
        for start, size in tiles_of(half_width):
            home_ref[:, start : start + size] = up_ref[:, start : start + size].astype(
                jnp.float32
            ) + pull_back(
                offset + start, dpre, stat_ref[:, :1], w_ref, x_ref, gain_ref, scale_ref, size, full_width
            )

    return pl.pallas_call(
        body,
        in_specs=[SCALAR] + [WHOLE] * 7,
        out_specs=[WHOLE, WHOLE],
        out_shape=[
            jax.ShapeDtypeStruct((rows, half_width), jnp.float32),
            pltpu.VMEM(weight.shape, weight.dtype),
        ],
        input_output_aliases={7: 1},
        compiler_params=pltpu.CompilerParams(vmem_limit_bytes=STEP_VMEM),
    )(core, upstream, dpre, stat, inputs, row_scale, gain, in_vmem(weight))


def adam(row_order, sides, features, dpre, masters, moment_one, moments, cuts):
    blocks, rows, first_width = moment_one.shape
    depth, width = dpre.shape
    counts = [len(pieces) for pieces in moments]
    parts, total = max(counts), sum(counts)
    strip = 16 if rows % 16 == 0 else rows
    fix_one = 1.0 - beta_one**step_count
    fix_two = 1.0 - beta_two**step_count

    def body(order_ref, side_ref, feature_ref, dpre_ref, *refs):
        w_refs, m_ref, refs = refs[: len(cuts)], refs[len(cuts)], refs[len(cuts) + 1 :]
        piece_refs, refs = refs[:total], refs[total:]
        new_w_ref, new_m_ref, new_v_ref, grad_ref, held_ref, sems = refs
        block = pl.program_id(0)

        def fetch(k):
            copies, start = [], 0
            for which in range(counts[k]):
                piece = piece_refs[sum(counts[:k]) + which]
                piece = piece.at[side_ref[k]] if k else piece
                end = start + piece.shape[-1]
                copies.append(
                    pltpu.make_async_copy(
                        piece, held_ref.at[k % 2, :, start:end], sems.at[which, k % 2]
                    )
                )
                start = end
            return copies

        @pl.when(block == 0)
        def _():
            for copy in fetch(0):
                copy.start()

        for k in range(blocks):

            @pl.when(block == k)
            def _(k=k):
                if k + 1 < blocks:
                    for copy in fetch(k + 1):
                        copy.start()

        grad_ref[...] = jnp.dot(feature_ref[0], dpre_ref[...], preferred_element_type=jnp.float32)

        for k in range(blocks):

            @pl.when(block == k)
            def _(k=k):
                for copy in fetch(k):
                    copy.wait()

        now = lax.rem(block, 2)

        def step(index, carry):
            part = pl.ds(index * strip, strip)
            for which, (lo, hi) in enumerate(cuts):
                grad = grad_ref[part, lo:hi]
                first = held_ref[now, part, width:] if which else m_ref[0, part, :]
                moment_next = beta_one * first.astype(jnp.float32) + (1.0 - beta_one) * grad
                second_next = (
                    beta_two * held_ref[now, part, lo:hi].astype(jnp.float32)
                    + (1.0 - beta_two) * grad * grad
                )
                scaled = second_next * (1.0 / fix_two)
                root = scaled * lax.rsqrt(scaled)
                direction = moment_next * pl.reciprocal(root + adam_eps, approx=True)
                rows_w = w_refs[which][0, part, :].astype(jnp.float32)
                new_w_ref[0, part, lo:hi] = (
                    rows_w * (1.0 - learn_rate * decay_rate) - (learn_rate / fix_one) * direction
                )
                new_m_ref[0, part, lo:hi] = moment_next.astype(jnp.bfloat16)
                new_v_ref[0, part, lo:hi] = second_next.astype(jnp.bfloat16)
            return carry

        lax.fori_loop(0, rows // strip, step, 0)

    def placed(i, order_ref, side_ref):
        return (order_ref[i], 0, 0)

    tile = pl.BlockSpec((1, rows, width), placed)
    return pl.pallas_call(
        body,
        grid_spec=pltpu.PrefetchScalarGridSpec(
            num_scalar_prefetch=2,
            grid=(blocks,),
            in_specs=[
                pl.BlockSpec((1, rows, depth), placed),
                pl.BlockSpec((depth, width), lambda i, o, s: (0, 0)),
            ]
            + [pl.BlockSpec((1, rows, hi - lo), placed) for lo, hi in cuts]
            + [pl.BlockSpec((1, rows, first_width), placed)]
            + [ANYWHERE] * total,
            out_specs=[tile, tile, tile],
            scratch_shapes=[
                pltpu.VMEM((rows, width), jnp.float32),
                pltpu.VMEM((2, rows, 2 * width - first_width), jnp.bfloat16),
                pltpu.SemaphoreType.DMA((parts, 2)),
            ],
        ),
        out_shape=[
            jax.ShapeDtypeStruct((blocks, rows, width), jnp.float32),
            jax.ShapeDtypeStruct((blocks, rows, width), jnp.bfloat16),
            jax.ShapeDtypeStruct((blocks, rows, width), jnp.bfloat16),
        ],
        compiler_params=pltpu.CompilerParams(vmem_limit_bytes=ADAM_VMEM),
    )(
        row_order,
        sides,
        features,
        dpre,
        *[in_hbm(piece) for piece in masters],
        in_hbm(moment_one),
        *[in_hbm(piece) for pieces in moments for piece in pieces],
    )


def local(old_w, old_m, old_v, old_slot_layer, norm_gain, tokens, cotangent):
    sections = lax.axis_size("section")
    replicas = lax.axis_size("dp")
    cores = lax.axis_size("mp")
    section_index = lax.axis_index("section")
    replica_index = lax.axis_index("dp")
    core_index = lax.axis_index("mp")
    full_width = tokens.shape[2]
    half_width = old_w.shape[4]
    row_block = sections * old_w.shape[3]
    tokens = tokens.reshape(-1, full_width)
    cotangent = cotangent.reshape(-1, full_width)
    token_total = tokens.shape[0]
    group_rows = token_total // GROUPS
    layer_ids = jnp.arange(sections, dtype=jnp.int32)
    matches = (old_slot_layer[None, :] == layer_ids[:, None]).astype(jnp.int32)
    inverse = jnp.sum(matches * layer_ids[None, :], axis=1)
    lanes = half_width // 128
    middle = lanes * FIRST_PART // 16 * 128
    cuts = [(0, middle), (middle, half_width)]
    sources = section_index ^ layer_ids
    sides = (section_index < sources).astype(jnp.int32)
    picks = jnp.take(inverse, sources)
    early = sections // 2
    breadth = 2 * half_width - middle
    edges = [breadth // 128 * part // PARTS * 128 for part in range(PARTS)] + [breadth]
    travelling = [(old_v, 0, half_width), (old_m, middle, half_width)]
    carried, sent = picked(picks[:early], inverse, travelling, [0, breadth], False)
    own_w = [relocate(piece) for piece in ordered_cast(carried, old_w, cuts)]
    blocks = [
        [turn(piece, "dp", by) if by else piece for piece in own_w] for by in range(replicas)
    ]

    def meet(piece, by):
        groups = [[s, s ^ by] for s in range(sections) if s < s ^ by]
        return lax.all_gather(piece, "section", axis=0, tiled=False, axis_index_groups=groups)

    moments = [sent[0]] + [[meet(piece, by) for piece in sent[by]] for by in range(1, early)]
    held = zero_after(blocks[-1][-1])
    _, ordered_m = picked(inverse + held, inverse, [(old_m, 0, middle)], [0, middle], True)
    moment_one = relocate(ordered_m)
    later = picks[early:] + zero_after(own_w[-1])
    _, sent = picked(later, inverse, travelling, edges, False)
    moments += [[meet(piece, by) for piece in sent[by - early]] for by in range(early, sections)]
    entry_section = section_index
    weight = resident((replica_index + zero_after(moment_one)).reshape(1), blocks, cuts)

    gain_row = norm_gain[0]

    def half_of(value, by=0):
        start = lax.rem(core_index + by, cores) * half_width
        return lax.dynamic_slice_in_dim(value, start, half_width, value.ndim - 1)

    def core_at(by):
        return lax.rem(core_index + by, cores).reshape(1)


    def put(stash, value, slot):
        return lax.dynamic_update_index_in_dim(stash, value, slot, 0)

    def get(stash, slot):
        return lax.dynamic_index_in_dim(stash, slot, 0, keepdims=False)

    def slot_of(group):
        return jnp.where((group >= 0) & (group < GROUPS), group, GROUPS)

    def hop(value, tick, by):
        senders = [tick - group for group in range(GROUPS) if 0 <= tick - group < sections - 1]
        pairs = [(s, s + 1) for s in senders]
        if by < 0:
            pairs = [(sections - 1 - s, sections - 2 - s) for s in senders]
        return lax.ppermute(value, "section", pairs)

    acts = jnp.zeros((GROUPS + 1, group_rows, full_width), jnp.bfloat16)
    norms = jnp.zeros((GROUPS + 1, group_rows, full_width), jnp.bfloat16)
    preacts = jnp.zeros((GROUPS + 1, group_rows, half_width), jnp.float32)
    slopes = jnp.zeros((GROUPS + 1, group_rows, half_width), jnp.float32)
    scales = jnp.zeros((GROUPS + 1, group_rows, 128), jnp.float32)
    dpres = jnp.zeros((GROUPS + 1, group_rows, half_width), jnp.bfloat16)
    ticks = GROUPS + sections - 1
    features = None
    forward_in = jnp.zeros((group_rows, full_width), jnp.bfloat16)
    backward_in = jnp.zeros((group_rows, half_width), jnp.bfloat16)

    def forward_tick(tick, arriving, stash, weight):
        acts, norms, preacts, slopes, scales = stash
        slot = slot_of(tick - section_index)
        inputs = arriving
        if tick < GROUPS:
            entry = tokens[tick * group_rows : (tick + 1) * group_rows]
            inputs = jnp.where(entry_section == 0, entry, arriving)
        output, normed, preact, scale, weight = forward_step(core_at(0), inputs, norm_gain, weight)
        sigmoid_value = jax.nn.sigmoid(preact)
        slope = sigmoid_value * (1.0 + preact * (1.0 - sigmoid_value))
        stash = (
            put(acts, inputs, slot),
            put(norms, normed, slot),
            put(preacts, preact, slot),
            put(slopes, slope, slot),
            put(scales, scale, slot),
        )
        if tick < ticks - 1:
            arriving = lax.all_gather(hop(output, tick, 1), "mp", axis=1, tiled=True)
        return arriving, stash, weight

    def backward_tick(tick, arriving, stash, dpres, weight):
        acts, _, preacts, slopes, scales = stash
        slot = slot_of(tick - (sections - 1 - section_index))
        slope, preact, inputs = get(slopes, slot), get(preacts, slot), get(acts, slot)
        row_scale = get(scales, slot)
        slope, preact, row_scale, inputs = lax.optimization_barrier(
            (slope, preact, row_scale, inputs)
        )
        upstream = arriving
        if tick < GROUPS:
            seed = cotangent[tick * group_rows : (tick + 1) * group_rows]
            upstream = jnp.where(section_index == sections - 1, half_of(seed), arriving)
        if tick == ticks - 1:
            dpre = (upstream.astype(jnp.float32) * slope).astype(jnp.bfloat16)
            return arriving, put(dpres, dpre, slot), weight
        for by in range(1, cores):
            dpre, stat, away, weight = backward_away(
                core_at(by), upstream, slope, preact, inputs, row_scale, norm_gain, weight
            )
            came = turn(away, "mp", by)
        home, weight = backward_home(
            core_at(0), upstream, dpre, stat, inputs, row_scale, norm_gain, weight
        )
        arriving = hop((home + came.astype(jnp.float32)).astype(jnp.bfloat16), tick, -1)
        return arriving, put(dpres, dpre, slot), weight

    stash = (acts, norms, preacts, slopes, scales)
    for tick in range(ticks - 1):
        forward_in, stash, weight = forward_tick(tick, forward_in, stash, weight)
    last_stash = stash
    for tick in range(ticks):
        if tick == 1:
            _, stash, weight = forward_tick(ticks - 1, forward_in, last_stash, weight)
        backward_in, dpres, weight = backward_tick(tick, backward_in, stash, dpres, weight)
        if tick == ticks - 2:
            settled = dpres[: GROUPS - 1].reshape(-1, half_width)
        if tick == GROUPS:
            block_start = replica_index
            normed_all = stash[1][:GROUPS].reshape(token_total, full_width)
            features = []
            for by in range(replicas):
                block = lax.rem(block_start + by, replicas) * row_block
                part = lax.dynamic_slice_in_dim(normed_all, block, row_block, 1)
                features.append(turn(part, "dp", by) if by else part)
            features = jnp.concatenate(features, axis=0)
            features = features.T.reshape(sections, -1, replicas * token_total)

    gathered = []
    for by in range(replicas):
        for part in (settled, dpres[GROUPS - 1]):
            gathered.append(turn(part, "dp", by) if by else part)
    blocked = (sections, -1)
    updated = adam(
        sources,
        sides,
        features,
        jnp.concatenate(gathered, axis=0),
        [piece.reshape(blocked + piece.shape[1:]) for piece in own_w],
        moment_one.reshape(blocked + moment_one.shape[1:]),
        moments,
        cuts,
    )
    return tuple(value.reshape(1, row_block, half_width) for value in updated)


def solution(mesh):
    placed = (
        P(None, "dp", "section", None, "mp"),
        P(None, "dp", "section", None, "mp"),
        P(None, "dp", "section", None, "mp"),
        P(),
        P("section", None),
        P(None, "dp", None),
        P(None, "dp", None),
    )
    return jax.shard_map(
        local,
        mesh=mesh,
        in_specs=placed,
        out_specs=(P("section", "dp", "mp"), P("section", "dp", "mp"), P("section", "dp", "mp")),
        check_vma=False,
    )
```

```python
import jax
import jax.numpy as jnp
from jax import lax
from jax.experimental import pallas as pl
from jax.experimental.pallas import tpu as pltpu
from jax.sharding import PartitionSpec as P

eps_norm = 1e-05
beta_one = 0.9
beta_two = 0.95
learn_rate = 0.001
decay_rate = 0.1
adam_eps = 1e-08
step_count = 1000.0

GROUPS = 2

FIRST_PART = 8
PARTS = 2
STEP_VMEM = 16 * 1024 * 1024
ADAM_VMEM = 24 * 1024 * 1024


def turn(value, axis, by):
    count = lax.axis_size(axis)
    return lax.ppermute(value, axis, [(i, (i + by) % count) for i in range(count)])


def zero_after(value):
    first = lax.slice(value, (0,) * value.ndim, (1,) * value.ndim).reshape(())
    return jnp.minimum((first > 0).astype(jnp.int32), 0)


def relocate(pieces):
    moved = lax.all_to_all(pieces, "section", split_axis=0, concat_axis=2, tiled=True)
    return moved.reshape(-1, moved.shape[-1])


def ordered_cast(picks, pieces, cuts):
    slots, _, _, rows, width = pieces.shape

    def body(pick_ref, in_ref, *out_refs):
        for (lo, hi), out_ref in zip(cuts, out_refs):
            out_ref[...] = in_ref[:, :, :, :, lo:hi].astype(out_ref.dtype)

    return pl.pallas_call(
        body,
        out_shape=[
            jax.ShapeDtypeStruct((slots, 1, 1, rows, hi - lo), jnp.bfloat16) for lo, hi in cuts
        ],
        grid_spec=pltpu.PrefetchScalarGridSpec(
            num_scalar_prefetch=1,
            grid=(slots,),
            in_specs=[pl.BlockSpec((1, 1, 1, rows, width), lambda i, p: (p[i], 0, 0, 0, 0))],
            out_specs=[
                pl.BlockSpec((1, 1, 1, rows, hi - lo), lambda i, p: (i, 0, 0, 0, 0))
                for lo, hi in cuts
            ],
        ),
        compiler_params=pltpu.CompilerParams(vmem_limit_bytes=STEP_VMEM),
    )(picks, pieces)


def picked(picks, carry, sources, edges, stacked):
    rows = sources[0][0].shape[3]
    count = picks.shape[0]
    ends = [0]
    for _, lo, hi in sources:
        ends.append(ends[-1] + hi - lo)
    dtype = sources[0][0].dtype
    spans = list(zip(edges[:-1], edges[1:]))

    def body(pick_ref, carry_ref, *refs):
        in_refs, refs = refs[: len(sources)], refs[len(sources) :]
        carried_ref, out_refs, (held_ref, sems, out_sems) = refs[0], refs[1:-3], refs[-3:]
        incoming = [
            [
                pltpu.make_async_copy(
                    in_ref.at[pick_ref[i], 0, 0, :, lo:hi],
                    held_ref.at[i, :, ends[j] : ends[j + 1]],
                    sems.at[i, j],
                )
                for j, (in_ref, (_, lo, hi)) in enumerate(zip(in_refs, sources))
            ]
            for i in range(count)
        ]
        outgoing = [
            [
                pltpu.make_async_copy(
                    held_ref.at[i, :, lo:hi],
                    out_refs[0].at[i, 0, 0] if stacked else out_refs[i * len(spans) + j],
                    out_sems.at[i, j],
                )
                for j, (lo, hi) in enumerate(spans)
            ]
            for i in range(count)
        ]
        for copies in incoming:
            for copy in copies:
                copy.start()
        for i in range(carry_ref.shape[0]):
            carried_ref[i] = carry_ref[i]
        for arrive, leave in zip(incoming, outgoing):
            for copy in arrive:
                copy.wait()
            for copy in leave:
                copy.start()
        for copies in outgoing:
            for copy in copies:
                copy.wait()

    if stacked:
        shapes = [jax.ShapeDtypeStruct((count, 1, 1, rows, ends[-1]), dtype)]
    else:
        shapes = [jax.ShapeDtypeStruct((rows, hi - lo), dtype) for lo, hi in spans] * count
    carried, *pieces = pl.pallas_call(
        body,
        out_shape=[jax.ShapeDtypeStruct(carry.shape, carry.dtype)] + shapes,
        in_specs=[SCALAR, SCALAR] + [ANYWHERE] * len(sources),
        out_specs=[SCALAR] + [ANYWHERE] * len(shapes),
        scratch_shapes=[
            pltpu.VMEM((count, rows, ends[-1]), dtype),
            pltpu.SemaphoreType.DMA((count, len(sources))),
            pltpu.SemaphoreType.DMA((count, len(spans))),
        ],
        compiler_params=pltpu.CompilerParams(vmem_limit_bytes=STEP_VMEM),
    )(picks, carry, *[in_hbm(array) for array, _, _ in sources])
    if stacked:
        return carried, pieces[0]
    return carried, [pieces[i * len(spans) : (i + 1) * len(spans)] for i in range(count)]


def resident(replica, blocks, cuts):
    replicas = len(blocks)
    rows = blocks[0][0].shape[0]
    flat = [piece for line in blocks for piece in line]

    def body(replica_ref, *refs):
        piece_refs, out_ref, sems = refs[:-2], refs[-2], refs[-1]
        copies = []
        for index, piece_ref in enumerate(piece_refs):
            by, (lo, hi) = index // len(cuts), cuts[index % len(cuts)]
            owner = lax.rem(replica_ref[0] + replicas - by, replicas)
            start = pl.multiple_of(owner * rows, 16)
            copies.append(
                pltpu.make_async_copy(
                    piece_ref, out_ref.at[pl.ds(start, rows), lo:hi], sems.at[index]
                )
            )
        for copy in copies:
            copy.start()
        for copy in copies:
            copy.wait()

    return pl.pallas_call(
        body,
        out_shape=pltpu.VMEM((replicas * rows, cuts[-1][1]), flat[0].dtype),
        in_specs=[SCALAR] + [ANYWHERE] * len(flat),
        out_specs=pl.BlockSpec(memory_space=pltpu.VMEM),
        scratch_shapes=[pltpu.SemaphoreType.DMA((len(flat),))],
        compiler_params=pltpu.CompilerParams(vmem_limit_bytes=STEP_VMEM),
    )(replica, *[in_hbm(piece) for piece in flat])


def tiles_of(width):
    return [(start, min(256, width - start)) for start in range(0, width, 256)]


def in_vmem(array):
    return pltpu.with_memory_space_constraint(array, pltpu.VMEM)


def in_hbm(array):
    return pltpu.with_memory_space_constraint(array, pltpu.HBM)


WHOLE = pl.BlockSpec(memory_space=pltpu.VMEM)
SCALAR = pl.BlockSpec(memory_space=pltpu.SMEM)
ANYWHERE = pl.BlockSpec(memory_space=pl.ANY)


def forward_step(core, inputs, gain, weight):
    rows, full_width = inputs.shape
    half_width = weight.shape[1]

    def body(core_ref, x_ref, gain_ref, w_ref, out_ref, normed_ref, preact_ref, scale_ref, _):
        wide = x_ref[...].astype(jnp.float32)
        scale = lax.rsqrt(jnp.mean(wide * wide, axis=1, keepdims=True) + eps_norm)
        normed = (wide * scale * gain_ref[...]).astype(jnp.bfloat16)
        normed_ref[...] = normed
        scale_ref[...] = jnp.broadcast_to(scale, scale_ref.shape)
        offset = pl.multiple_of(core_ref[0] * half_width, 128)
        for start, size in tiles_of(half_width):
            preact = jnp.dot(
                normed, w_ref[:, start : start + size], preferred_element_type=jnp.float32
            )
            preact_ref[:, start : start + size] = preact
            own = x_ref[:, pl.ds(pl.multiple_of(offset + start, 128), size)].astype(jnp.float32)
            silu = preact / (1.0 + jnp.exp(-preact))
            out_ref[:, start : start + size] = (own + silu).astype(jnp.bfloat16)

    return pl.pallas_call(
        body,
        in_specs=[SCALAR, WHOLE, WHOLE, WHOLE],
        out_specs=[WHOLE] * 5,
        out_shape=[
            jax.ShapeDtypeStruct((rows, half_width), jnp.bfloat16),
            jax.ShapeDtypeStruct((rows, full_width), jnp.bfloat16),
            jax.ShapeDtypeStruct((rows, half_width), jnp.float32),
            jax.ShapeDtypeStruct((rows, 128), jnp.float32),
            pltpu.VMEM(weight.shape, weight.dtype),
        ],
        input_output_aliases={3: 4},
        compiler_params=pltpu.CompilerParams(vmem_limit_bytes=STEP_VMEM),
    )(core, inputs, gain, in_vmem(weight))


def pull_back(start, dpre, stat, w_ref, x_ref, gain_ref, scale_ref, size, width):
    cols = pl.ds(pl.multiple_of(start, 128), size)
    product = lax.dot_general(
        dpre, w_ref[cols, :], (((1,), (1,)), ((), ())), preferred_element_type=jnp.float32
    )
    scale = scale_ref[:, :1]
    return scale * (
        gain_ref[:, cols] * product - x_ref[:, cols].astype(jnp.float32) * (scale * stat / width)
    )


def backward_away(core, upstream, slope, preact, inputs, row_scale, gain, weight):
    rows, full_width = inputs.shape
    half_width = weight.shape[1]

    def body(
        core_ref, up_ref, slope_ref, preact_ref, x_ref, scale_ref, gain_ref, w_ref,
        dpre_ref, stat_ref, away_ref, _,
    ):
        dpre = (up_ref[...].astype(jnp.float32) * slope_ref[...]).astype(jnp.bfloat16)
        dpre_ref[...] = dpre
        stat = jnp.sum(dpre.astype(jnp.float32) * preact_ref[...], axis=1, keepdims=True)
        stat_ref[...] = jnp.broadcast_to(stat, stat_ref.shape)
        offset = pl.multiple_of(core_ref[0] * half_width, 128)
        for start, size in tiles_of(half_width):
            away_ref[:, start : start + size] = pull_back(
                offset + start, dpre, stat, w_ref, x_ref, gain_ref, scale_ref, size, full_width
            ).astype(jnp.bfloat16)

    return pl.pallas_call(
        body,
        in_specs=[SCALAR] + [WHOLE] * 7,
        out_specs=[WHOLE] * 4,
        out_shape=[
            jax.ShapeDtypeStruct((rows, half_width), jnp.bfloat16),
            jax.ShapeDtypeStruct((rows, 128), jnp.float32),
            jax.ShapeDtypeStruct((rows, half_width), jnp.bfloat16),
            pltpu.VMEM(weight.shape, weight.dtype),
        ],
        input_output_aliases={7: 3},
        compiler_params=pltpu.CompilerParams(vmem_limit_bytes=STEP_VMEM),
    )(core, upstream, slope, preact, inputs, row_scale, gain, in_vmem(weight))


def backward_home(core, upstream, dpre, stat, inputs, row_scale, gain, weight):
    rows, full_width = inputs.shape
    half_width = weight.shape[1]

    def body(core_ref, up_ref, dpre_ref, stat_ref, x_ref, scale_ref, gain_ref, w_ref, home_ref, _):
        dpre = dpre_ref[...]
        offset = pl.multiple_of(core_ref[0] * half_width, 128)
        for start, size in tiles_of(half_width):
            home_ref[:, start : start + size] = up_ref[:, start : start + size].astype(
                jnp.float32
            ) + pull_back(
                offset + start, dpre, stat_ref[:, :1], w_ref, x_ref, gain_ref, scale_ref, size, full_width
            )

    return pl.pallas_call(
        body,
        in_specs=[SCALAR] + [WHOLE] * 7,
        out_specs=[WHOLE, WHOLE],
        out_shape=[
            jax.ShapeDtypeStruct((rows, half_width), jnp.float32),
            pltpu.VMEM(weight.shape, weight.dtype),
        ],
        input_output_aliases={7: 1},
        compiler_params=pltpu.CompilerParams(vmem_limit_bytes=STEP_VMEM),
    )(core, upstream, dpre, stat, inputs, row_scale, gain, in_vmem(weight))


def adam(row_order, sides, features, dpre, masters, moment_one, moments, cuts):
    blocks, rows, first_width = moment_one.shape
    depth, width = dpre.shape
    counts = [len(pieces) for pieces in moments]
    parts, total = max(counts), sum(counts)
    strip = 16 if rows % 16 == 0 else rows
    fix_one = 1.0 - beta_one**step_count
    fix_two = 1.0 - beta_two**step_count

    def body(order_ref, side_ref, feature_ref, dpre_ref, *refs):
        w_refs, m_ref, refs = refs[: len(cuts)], refs[len(cuts)], refs[len(cuts) + 1 :]
        piece_refs, refs = refs[:total], refs[total:]
        new_w_ref, new_m_ref, new_v_ref, grad_ref, held_ref, sems = refs
        block = pl.program_id(0)

        def fetch(k):
            copies, start = [], 0
            for which in range(counts[k]):
                piece = piece_refs[sum(counts[:k]) + which]
                piece = piece.at[side_ref[k]] if k else piece
                end = start + piece.shape[-1]
                copies.append(
                    pltpu.make_async_copy(
                        piece, held_ref.at[k % 2, :, start:end], sems.at[which, k % 2]
                    )
                )
                start = end
            return copies

        @pl.when(block == 0)
        def _():
            for copy in fetch(0):
                copy.start()

        for k in range(blocks):

            @pl.when(block == k)
            def _(k=k):
                if k + 1 < blocks:
                    for copy in fetch(k + 1):
                        copy.start()

        grad_ref[...] = jnp.dot(feature_ref[0], dpre_ref[...], preferred_element_type=jnp.float32)

        for k in range(blocks):

            @pl.when(block == k)
            def _(k=k):
                for copy in fetch(k):
                    copy.wait()

        now = lax.rem(block, 2)

        def step(index, carry):
            part = pl.ds(index * strip, strip)
            for which, (lo, hi) in enumerate(cuts):
                grad = grad_ref[part, lo:hi]
                first = held_ref[now, part, width:] if which else m_ref[0, part, :]
                moment_next = beta_one * first.astype(jnp.float32) + (1.0 - beta_one) * grad
                second_next = (
                    beta_two * held_ref[now, part, lo:hi].astype(jnp.float32)
                    + (1.0 - beta_two) * grad * grad
                )
                scaled = second_next * (1.0 / fix_two)
                root = scaled * lax.rsqrt(scaled)
                direction = moment_next * pl.reciprocal(root + adam_eps, approx=True)
                rows_w = w_refs[which][0, part, :].astype(jnp.float32)
                new_w_ref[0, part, lo:hi] = (
                    rows_w * (1.0 - learn_rate * decay_rate) - (learn_rate / fix_one) * direction
                )
                new_m_ref[0, part, lo:hi] = moment_next.astype(jnp.bfloat16)
                new_v_ref[0, part, lo:hi] = second_next.astype(jnp.bfloat16)
            return carry

        lax.fori_loop(0, rows // strip, step, 0)

    def placed(i, order_ref, side_ref):
        return (order_ref[i], 0, 0)

    tile = pl.BlockSpec((1, rows, width), placed)
    return pl.pallas_call(
        body,
        grid_spec=pltpu.PrefetchScalarGridSpec(
            num_scalar_prefetch=2,
            grid=(blocks,),
            in_specs=[
                pl.BlockSpec((1, rows, depth), placed),
                pl.BlockSpec((depth, width), lambda i, o, s: (0, 0)),
            ]
            + [pl.BlockSpec((1, rows, hi - lo), placed) for lo, hi in cuts]
            + [pl.BlockSpec((1, rows, first_width), placed)]
            + [ANYWHERE] * total,
            out_specs=[tile, tile, tile],
            scratch_shapes=[
                pltpu.VMEM((rows, width), jnp.float32),
                pltpu.VMEM((2, rows, 2 * width - first_width), jnp.bfloat16),
                pltpu.SemaphoreType.DMA((parts, 2)),
            ],
        ),
        out_shape=[
            jax.ShapeDtypeStruct((blocks, rows, width), jnp.float32),
            jax.ShapeDtypeStruct((blocks, rows, width), jnp.bfloat16),
            jax.ShapeDtypeStruct((blocks, rows, width), jnp.bfloat16),
        ],
        compiler_params=pltpu.CompilerParams(vmem_limit_bytes=ADAM_VMEM),
    )(
        row_order,
        sides,
        features,
        dpre,
        *[in_hbm(piece) for piece in masters],
        in_hbm(moment_one),
        *[in_hbm(piece) for pieces in moments for piece in pieces],
    )


def local(old_w, old_m, old_v, old_slot_layer, norm_gain, tokens, cotangent):
    sections = lax.axis_size("section")
    replicas = lax.axis_size("dp")
    cores = lax.axis_size("mp")
    section_index = lax.axis_index("section")
    replica_index = lax.axis_index("dp")
    core_index = lax.axis_index("mp")
    full_width = tokens.shape[2]
    half_width = old_w.shape[4]
    row_block = sections * old_w.shape[3]
    tokens = tokens.reshape(-1, full_width)
    cotangent = cotangent.reshape(-1, full_width)
    token_total = tokens.shape[0]
    group_rows = token_total // GROUPS
    layer_ids = jnp.arange(sections, dtype=jnp.int32)
    matches = (old_slot_layer[None, :] == layer_ids[:, None]).astype(jnp.int32)
    inverse = jnp.sum(matches * layer_ids[None, :], axis=1)
    lanes = half_width // 128
    middle = lanes * FIRST_PART // 16 * 128
    cuts = [(0, middle), (middle, half_width)]
    sources = section_index ^ layer_ids
    sides = (section_index < sources).astype(jnp.int32)
    picks = jnp.take(inverse, sources)
    early = sections // 2
    breadth = 2 * half_width - middle
    edges = [breadth // 128 * part // PARTS * 128 for part in range(PARTS)] + [breadth]
    travelling = [(old_v, 0, half_width), (old_m, middle, half_width)]
    carried, sent = picked(picks[:early], inverse, travelling, [0, breadth], False)
    own_w = [relocate(piece) for piece in ordered_cast(carried, old_w, cuts)]
    blocks = [
        [turn(piece, "dp", by) if by else piece for piece in own_w] for by in range(replicas)
    ]

    def meet(piece, by):
        groups = [[s, s ^ by] for s in range(sections) if s < s ^ by]
        return lax.all_gather(piece, "section", axis=0, tiled=False, axis_index_groups=groups)

    moments = [sent[0]] + [[meet(piece, by) for piece in sent[by]] for by in range(1, early)]
    held = zero_after(blocks[-1][-1])
    _, ordered_m = picked(inverse + held, inverse, [(old_m, 0, middle)], [0, middle], True)
    moment_one = relocate(ordered_m)
    later = picks[early:] + zero_after(own_w[-1])
    _, sent = picked(later, inverse, travelling, edges, False)
    crossing = {
        by: [meet(piece, by) for piece in sent[by - early]]
        for by in sorted(range(early, sections), key=lambda by: (1 - by % 2, by))
    }
    moments += [crossing[by] for by in range(early, sections)]
    entry_section = section_index
    weight = resident((replica_index + zero_after(moment_one)).reshape(1), blocks, cuts)

    gain_row = norm_gain[0]

    def half_of(value, by=0):
        start = lax.rem(core_index + by, cores) * half_width
        return lax.dynamic_slice_in_dim(value, start, half_width, value.ndim - 1)

    def core_at(by):
        return lax.rem(core_index + by, cores).reshape(1)


    def put(stash, value, slot):
        return lax.dynamic_update_index_in_dim(stash, value, slot, 0)

    def get(stash, slot):
        return lax.dynamic_index_in_dim(stash, slot, 0, keepdims=False)

    def slot_of(group):
        return jnp.where((group >= 0) & (group < GROUPS), group, GROUPS)

    def hop(value, tick, by):
        senders = [tick - group for group in range(GROUPS) if 0 <= tick - group < sections - 1]
        pairs = [(s, s + 1) for s in senders]
        if by < 0:
            pairs = [(sections - 1 - s, sections - 2 - s) for s in senders]
        return lax.ppermute(value, "section", pairs)

    acts = jnp.zeros((GROUPS + 1, group_rows, full_width), jnp.bfloat16)
    norms = jnp.zeros((GROUPS + 1, group_rows, full_width), jnp.bfloat16)
    preacts = jnp.zeros((GROUPS + 1, group_rows, half_width), jnp.float32)
    slopes = jnp.zeros((GROUPS + 1, group_rows, half_width), jnp.float32)
    scales = jnp.zeros((GROUPS + 1, group_rows, 128), jnp.float32)
    dpres = jnp.zeros((GROUPS + 1, group_rows, half_width), jnp.bfloat16)
    ticks = GROUPS + sections - 1
    features = None
    forward_in = jnp.zeros((group_rows, full_width), jnp.bfloat16)
    backward_in = jnp.zeros((group_rows, half_width), jnp.bfloat16)

    def forward_tick(tick, arriving, stash, weight):
        acts, norms, preacts, slopes, scales = stash
        slot = slot_of(tick - section_index)
        inputs = arriving
        if tick < GROUPS:
            entry = tokens[tick * group_rows : (tick + 1) * group_rows]
            inputs = jnp.where(entry_section == 0, entry, arriving)
        output, normed, preact, scale, weight = forward_step(core_at(0), inputs, norm_gain, weight)
        sigmoid_value = jax.nn.sigmoid(preact)
        slope = sigmoid_value * (1.0 + preact * (1.0 - sigmoid_value))
        stash = (
            put(acts, inputs, slot),
            put(norms, normed, slot),
            put(preacts, preact, slot),
            put(slopes, slope, slot),
            put(scales, scale, slot),
        )
        if tick < ticks - 1:
            arriving = lax.all_gather(hop(output, tick, 1), "mp", axis=1, tiled=True)
        return arriving, stash, weight

    def backward_tick(tick, arriving, stash, dpres, weight):
        acts, _, preacts, slopes, scales = stash
        slot = slot_of(tick - (sections - 1 - section_index))
        slope, preact, inputs = get(slopes, slot), get(preacts, slot), get(acts, slot)
        row_scale = get(scales, slot)
        slope, preact, row_scale, inputs = lax.optimization_barrier(
            (slope, preact, row_scale, inputs)
        )
        upstream = arriving
        if tick < GROUPS:
            seed = cotangent[tick * group_rows : (tick + 1) * group_rows]
            upstream = jnp.where(section_index == sections - 1, half_of(seed), arriving)
        if tick == ticks - 1:
            dpre = (upstream.astype(jnp.float32) * slope).astype(jnp.bfloat16)
            return arriving, put(dpres, dpre, slot), weight
        for by in range(1, cores):
            dpre, stat, away, weight = backward_away(
                core_at(by), upstream, slope, preact, inputs, row_scale, norm_gain, weight
            )
            came = turn(away, "mp", by)
        home, weight = backward_home(
            core_at(0), upstream, dpre, stat, inputs, row_scale, norm_gain, weight
        )
        arriving = hop((home + came.astype(jnp.float32)).astype(jnp.bfloat16), tick, -1)
        return arriving, put(dpres, dpre, slot), weight

    stash = (acts, norms, preacts, slopes, scales)
    for tick in range(ticks - 1):
        forward_in, stash, weight = forward_tick(tick, forward_in, stash, weight)
    last_stash = stash
    for tick in range(ticks):
        if tick == 1:
            _, stash, weight = forward_tick(ticks - 1, forward_in, last_stash, weight)
        backward_in, dpres, weight = backward_tick(tick, backward_in, stash, dpres, weight)
        if tick == ticks - 2:
            settled = dpres[: GROUPS - 1].reshape(-1, half_width)
        if tick == GROUPS:
            block_start = replica_index
            normed_all = stash[1][:GROUPS].reshape(token_total, full_width)
            features = []
            for by in range(replicas):
                block = lax.rem(block_start + by, replicas) * row_block
                part = lax.dynamic_slice_in_dim(normed_all, block, row_block, 1)
                features.append(turn(part, "dp", by) if by else part)
            features = jnp.concatenate(features, axis=0)
            features = features.T.reshape(sections, -1, replicas * token_total)

    gathered = []
    for by in range(replicas):
        for part in (settled, dpres[GROUPS - 1]):
            gathered.append(turn(part, "dp", by) if by else part)
    blocked = (sections, -1)
    updated = adam(
        sources,
        sides,
        features,
        jnp.concatenate(gathered, axis=0),
        [piece.reshape(blocked + piece.shape[1:]) for piece in own_w],
        moment_one.reshape(blocked + moment_one.shape[1:]),
        moments,
        cuts,
    )
    return tuple(value.reshape(1, row_block, half_width) for value in updated)


def solution(mesh):
    placed = (
        P(None, "dp", "section", None, "mp"),
        P(None, "dp", "section", None, "mp"),
        P(None, "dp", "section", None, "mp"),
        P(),
        P("section", None),
        P(None, "dp", None),
        P(None, "dp", None),
    )
    return jax.shard_map(
        local,
        mesh=mesh,
        in_specs=placed,
        out_specs=(P("section", "dp", "mp"), P("section", "dp", "mp"), P("section", "dp", "mp")),
        check_vma=False,
    )
```
